32 devices in a mesh: expert: 16 (over z, y, core), dp: 2 (over x).
Axes of the slice: x: 2, y: 2, z: 4, core: 2. Of those that a mesh axis runs over, the one named last changes fastest.
Arguments:
- tokens: bfloat16 [2048, 2048], P('expert', 'dp'), may hold values from -6 to 6
- grad_out: bfloat16 [2048, 2048], P('expert', 'dp'), may hold values from -6 to 6
- routes: int32 [2048, 8], P('expert'), may hold values from 0 to 15, all different within a row; in each aligned block of 128 rows (0 to 127, 128 to 255, ...) at most 96 rows name the same one
- gates: float32 [2048, 8], P('expert'), may hold values from 0.1 to 1
- w_gate: bfloat16 [16, 2048, 384], P('expert', 'dp'), may hold values from -0.125 to 0.125
- w_up: bfloat16 [16, 2048, 384], P('expert', 'dp'), may hold values from -0.125 to 0.125
- w_down: bfloat16 [16, 384, 2048], P('expert', None, 'dp'), may hold values from -0.3125 to 0.3125
Outputs:
- d_tokens: bfloat16 [2048, 2048], P('expert', 'dp')
- grad_gate: bfloat16 [16, 2048, 384], P('expert', 'dp')
- grad_up: bfloat16 [16, 2048, 384], P('expert', 'dp')
- grad_down: bfloat16 [16, 384, 2048], P('expert', None, 'dp')
The draws below stay inside these ranges and needn't reach their ends.
Inputs may be any that keep to these rules, and one draw needn't show every extreme that they name: `routes`: each row names 8 different experts; in each aligned block of 128 rows no expert is named by more than 96 rows, a bound that some block reaches.
All inputs are finite; a program needn't handle non-finite values.
Results may differ from the reference program's by a relative error of at most 0.013.
Values may be sent and summed in bfloat16 or wider, within the bound.
A program may use at most 64 MiB of HBM per device.

```python
import math
import jax
import jax.numpy as jnp
import numpy as np
from jax import lax

D = 2048
TOP = 8
FW = 384
TOK_DEV = 128
EXPERTS = 16
MOST = 96
TOKENS = 2048
N_EXPERT = 16
N_DP = 2


def steps_of(stream_key, extent, split, least, largest):
    level, own = 1.0, jax.random.fold_in(stream_key, 6)
    for dim, parts in split:
        heights = jnp.exp(jax.random.uniform(jax.random.fold_in(own, dim), (parts,), jnp.float32, least / len(split), largest / len(split)))
        level = level * jnp.repeat(heights, extent[dim] // parts).reshape([-1 if axis == dim else 1 for axis in range(len(extent))])
    return level


def assign_block(stream_key, own, number, rows, count, top, bound, skew):
    order = jax.random.permutation(stream_key, count)
    crowded, common = load_shares(count, rows * top, bound, skew, True), load_shares(count, rows * top, bound, skew, False)
    places = jnp.arange(count)

    def named(sizes, turn):
        used = int((sizes > 0).sum())
        fixed = max(1, used // 4)
        moved = fixed + (places - fixed + turn * (used - fixed)) % max(1, count - fixed)
        return jnp.zeros((count,), jnp.int32).at[order[jnp.where(places < fixed, places, moved)]].set(jnp.asarray(sizes, jnp.int32))

    sizes = jnp.where(number % 4 == 0, named(crowded, number // 4), named(common, number - number // 4 - 1))
    mixed = jax.random.permutation(jax.random.fold_in(own, 3), count)
    giver, sink = mixed[0:count // 2 * 2:2], mixed[1:count // 2 * 2:2]
    room = jnp.minimum(sizes[giver] - 1, bound - sizes[sink]) // 2
    room = jnp.where((giver == order[0]) | (sink == order[0]) | (sizes[sink] == 0), 0, jnp.maximum(room, 0))
    moved = jax.random.randint(jax.random.fold_in(own, 4), (count // 2,), 0, 1 << 20) % (room + 1)
    sizes = sizes.at[giver].add(-moved).at[sink].add(moved)
    members = jnp.searchsorted(jnp.cumsum(sizes), jnp.arange(rows * top), side="right").astype(jnp.int32)
    table = members.reshape(top, rows).T
    table = table[jax.random.permutation(jax.random.fold_in(own, 1), rows)]
    turn = jax.random.randint(jax.random.fold_in(own, 2), (rows, 1), 0, top)
    return jnp.take_along_axis(table, (jnp.arange(top)[None, :] + turn) % top, axis=1)


def load_shares(count, total, most, slope, full):
    loads = [(1 << 20) // math.isqrt(rank ** slope) + 1 for rank in range(1, count + 1)]
    largest = most if full else min(most, max(-(-total // count), total * loads[0] // sum(loads)))
    least = 1 if total - largest >= count - 1 else 0
    holding, rest = [largest] + [least] * (count - 1), total - largest - least * (count - 1)
    while rest > 0:
        candidates = [i for i in range(1, count) if holding[i] < largest] or [i for i in range(1, count) if holding[i] < most]
        whole, budget = sum([loads[i] for i in candidates]), rest
        for i in candidates:
            addition = min(most - holding[i], max(1, budget * loads[i] // whole), rest)
            holding[i] = holding[i] + addition
            rest = rest - addition
    return np.array(holding)


def scatter_about(stream_key, dims, scale, bound, shards=(), kind=jnp.bfloat16):
    level = steps_of(stream_key, dims, shards, -0.22, 0.18) if shards else 1.0
    result = jax.random.normal(stream_key, dims, jnp.float32) * scale * level
    return jnp.minimum(jnp.maximum(result, -bound), bound).astype(kind)


def setup_inputs(seed: int = 0) -> dict:
    keys = jax.random.split(jax.random.key(seed), 8)
    tokens = scatter_about(keys[0], (TOKENS, D), 1.0, 6.0, ((0, 16), (1, 2)))
    grad_out = scatter_about(keys[1], (TOKENS, D), 1.0, 6.0, ((0, 16), (1, 2)))
    routes_keys = jax.random.split(jax.random.fold_in(keys[2], 1), TOKENS // TOK_DEV)
    routes_turns = jax.random.permutation(jax.random.fold_in(keys[2], 3), TOKENS // TOK_DEV)
    routes = jax.vmap(lambda own, number: assign_block(jax.random.fold_in(keys[2], 2), own, number, TOK_DEV, EXPERTS, TOP, MOST, 2))(routes_keys, routes_turns).reshape((TOKENS, TOP))
    gates = jnp.clip(jnp.exp(math.log(1.0) - 2.3025851 * jax.random.uniform(keys[3], (TOKENS, TOP), jnp.float32) ** steps_of(keys[3], (TOKENS, TOP), ((0, 16),), -0.2, 0.2)), 0.1, 1.0)
    w_gate = scatter_about(keys[4], (EXPERTS, D, FW), D ** -0.5, 0.125, ((0, 16), (1, 2)))
    w_up = scatter_about(keys[5], (EXPERTS, D, FW), D ** -0.5, 0.125, ((0, 16), (1, 2)))
    w_down = scatter_about(keys[6], (EXPERTS, FW, D), FW ** -0.5, 0.3125, ((0, 16), (2, 2)))
    return {"tokens": tokens, "grad_out": grad_out, "routes": routes, "gates": gates, "w_gate": w_gate, "w_up": w_up, "w_down": w_down}


def split_round(left_rows, right_rows, member):
    masked = right_rows.astype(jnp.float32)[None, :, :] * member.T[:, :, None]
    partial_value = jnp.einsum("ra,jrb->jab", left_rows.astype(jnp.float32), masked)
    rounded = lax.optimization_barrier(partial_value.astype(jnp.bfloat16))
    return jnp.sum(rounded.astype(jnp.float32), axis=0).astype(jnp.bfloat16)


def reference(tokens, grad_out, routes, gates, w_gate, w_up, w_down):
    flat_routes = routes.reshape(-1).astype(jnp.int32)
    flat_gates = gates.reshape(-1)
    row_total = TOKENS * TOP
    capacity = N_EXPERT * MOST
    model_width = tokens.shape[1]
    group_width = N_EXPERT // N_DP

    def one_expert(accum, expert_id):
        found = jnp.nonzero(flat_routes == expert_id, size=capacity, fill_value=row_total)[0].astype(jnp.int32)
        valid = found < row_total
        safe_rows = jnp.where(valid, found, 0).astype(jnp.int32)
        token_ids = (safe_rows // TOP).astype(jnp.int32)
        replica = ((token_ids // TOK_DEV) // group_width).astype(jnp.int32)
        member = ((replica[:, None] == jnp.arange(N_DP, dtype=jnp.int32)[None, :]) & valid[:, None]).astype(jnp.float32)
        inputs = jnp.where(valid[:, None], tokens[token_ids], jnp.zeros((), tokens.dtype))
        scaled = jnp.where(valid[:, None], grad_out[token_ids].astype(jnp.float32) * flat_gates[safe_rows][:, None], 0.0).astype(jnp.bfloat16)
        wg = w_gate[expert_id]
        wu = w_up[expert_id]
        wd = w_down[expert_id]
        pre_gate = jnp.dot(inputs, wg, preferred_element_type=jnp.float32)
        pre_up = jnp.dot(inputs, wu, preferred_element_type=jnp.float32)
        sigmoid_gate = jax.nn.sigmoid(pre_gate)
        activated = pre_gate * sigmoid_gate
        hidden = (activated * pre_up).astype(jnp.bfloat16)
        back_hidden = jnp.dot(scaled, wd.T, preferred_element_type=jnp.float32)
        d_up = (back_hidden * activated).astype(jnp.bfloat16)
        d_gate = (back_hidden * pre_up * sigmoid_gate * (1.0 + pre_gate * (1.0 - sigmoid_gate))).astype(jnp.bfloat16)
        row_grad = (jnp.dot(d_gate, wg.T, preferred_element_type=jnp.float32) + jnp.dot(d_up, wu.T, preferred_element_type=jnp.float32)).astype(jnp.bfloat16)
        contrib = jnp.where(valid[:, None], row_grad.astype(jnp.float32), 0.0)
        accum = accum.at[token_ids].add(contrib)
        grads = (split_round(inputs, d_gate, member), split_round(inputs, d_up, member), split_round(hidden, scaled, member))
        return accum, grads

    start = jnp.zeros((TOKENS, model_width), jnp.float32)
    accum, grads = lax.scan(one_expert, start, jnp.arange(EXPERTS, dtype=jnp.int32))
    return accum.astype(jnp.bfloat16), grads[0], grads[1], grads[2]
```

```python
import jax
import jax.numpy as jnp
from jax import lax
from jax.sharding import PartitionSpec as P


def contract_rows(left_rows, right_rows):
    return lax.dot_general(
        left_rows, right_rows, (((0,), (0,)), ((), ())), preferred_element_type=jnp.float32
    )


def contract_cols(left_rows, right_rows):
    return lax.dot_general(
        left_rows, right_rows, (((1,), (1,)), ((), ())), preferred_element_type=jnp.float32
    )


def per_source(left_rows, right_rows, dp_count):
    left_split = left_rows.reshape(dp_count, -1, left_rows.shape[1])
    right_split = right_rows.reshape(dp_count, -1, right_rows.shape[1])
    partial_value = jnp.einsum(
        "jra,jrb->jab", left_split, right_split, preferred_element_type=jnp.float32
    )
    rounded = lax.optimization_barrier(partial_value.astype(jnp.bfloat16))
    return jnp.sum(rounded.astype(jnp.float32), axis=0).astype(jnp.bfloat16)


def shards(tokens, grad_out, routes, gates, w_gate, w_up, w_down):
    experts = lax.axis_size("expert")
    dp_count = lax.axis_size("dp")
    tok_count = tokens.shape[0]
    top_count = routes.shape[1]
    slot_cap = min(tok_count, max(2, 3 * tok_count * top_count // (2 * experts)))
    row_total = tok_count * top_count
    flat_routes = routes.reshape(-1)
    flat_gates = gates.reshape(-1)
    onehot = (flat_routes[:, None] == jnp.arange(experts, dtype=jnp.int32)[None, :]).astype(
        jnp.int32
    )
    slot_rank = jnp.sum((jnp.cumsum(onehot, axis=0) - onehot) * onehot, axis=1)
    slot_index = flat_routes * slot_cap + slot_rank
    slot_source = (
        jnp.full((experts * slot_cap,), row_total, jnp.int32)
        .at[slot_index]
        .set(jnp.arange(row_total, dtype=jnp.int32))
    )
    valid = slot_source < row_total
    safe_rows = jnp.where(valid, slot_source, 0)
    token_ids = safe_rows // top_count
    token_slots = jnp.where(valid[:, None], tokens[token_ids], jnp.zeros((), tokens.dtype))
    scaled_slots = jnp.where(
        valid[:, None],
        grad_out[token_ids].astype(jnp.float32) * flat_gates[safe_rows][:, None],
        0.0,
    ).astype(jnp.bfloat16)
    input_cols, scaled_cols = (
        lax.all_to_all(token_slots, "expert", split_axis=0, concat_axis=0, tiled=True),
        lax.all_to_all(scaled_slots, "expert", split_axis=0, concat_axis=0, tiled=True),
    )
    inputs, scaled = (
        lax.all_to_all(input_cols, "dp", split_axis=0, concat_axis=1, tiled=True),
        lax.all_to_all(scaled_cols, "dp", split_axis=0, concat_axis=1, tiled=True),
    )
    full_gate, full_up, full_down = (
        lax.all_gather(w_gate, "dp", axis=1, tiled=True),
        lax.all_gather(w_up, "dp", axis=1, tiled=True),
        lax.all_gather(w_down, "dp", axis=2, tiled=True),
    )
    full_gate = full_gate[0]
    full_up = full_up[0]
    full_down = full_down[0]
    pre_gate = jnp.dot(inputs, full_gate, preferred_element_type=jnp.float32)
    pre_up = jnp.dot(inputs, full_up, preferred_element_type=jnp.float32)
    sigmoid_gate = jax.nn.sigmoid(pre_gate)
    activated = pre_gate * sigmoid_gate
    hidden = (activated * pre_up).astype(jnp.bfloat16)
    back_hidden = contract_cols(scaled, full_down)
    d_up = (back_hidden * activated).astype(jnp.bfloat16)
    d_gate = (back_hidden * pre_up * sigmoid_gate * (1.0 + pre_gate * (1.0 - sigmoid_gate))).astype(
        jnp.bfloat16
    )
    row_grad = (contract_cols(d_gate, full_gate) + contract_cols(d_up, full_up)).astype(
        jnp.bfloat16
    )
    came_back = lax.all_to_all(
        lax.all_to_all(row_grad, "dp", split_axis=1, concat_axis=0, tiled=True),
        "expert",
        split_axis=0,
        concat_axis=0,
        tiled=True,
    )
    picked = came_back[slot_index].astype(jnp.float32)
    d_tokens = jnp.sum(picked.reshape(tok_count, top_count, -1), axis=1).astype(jnp.bfloat16)
    hidden_all = lax.all_gather(hidden, "dp", axis=0, tiled=True)
    grad_down = per_source(hidden_all, scaled_cols, dp_count)
    gate_part = contract_rows(inputs, d_gate).astype(jnp.bfloat16).astype(jnp.float32)
    up_part = contract_rows(inputs, d_up).astype(jnp.bfloat16).astype(jnp.float32)
    gate_sum, up_sum = (
        lax.psum_scatter(
            gate_part.astype(jnp.bfloat16), "dp", scatter_dimension=0, tiled=True
        ).astype(jnp.float32),
        lax.psum_scatter(
            up_part.astype(jnp.bfloat16), "dp", scatter_dimension=0, tiled=True
        ).astype(jnp.float32),
    )
    grad_gate = gate_sum.astype(jnp.bfloat16)
    grad_up = up_sum.astype(jnp.bfloat16)
    return (d_tokens, grad_gate[None], grad_up[None], grad_down[None])


def dense_shards(tokens, grad_out, routes, gates, w_gate, w_up, w_down):
    experts = lax.axis_size("expert")
    dp_count = lax.axis_size("dp")
    me = lax.axis_index("expert")
    mine = lax.axis_index("dp")
    half = tokens.shape[0] // dp_count
    named = routes[:, :, None] == jnp.arange(experts, dtype=jnp.int32)
    table = jnp.sum(jnp.where(named, gates[:, :, None], 0.0), axis=1)
    table = lax.dynamic_slice_in_dim(table, mine * half, half, axis=0)
    table = lax.all_gather(table, "expert", axis=0, tiled=True)
    weight = jnp.sum(jnp.where(jnp.arange(experts)[None, :] == me, table, 0.0), axis=1)[:, None]
    inputs = lax.all_to_all(tokens, "dp", split_axis=0, concat_axis=1, tiled=True)
    cotangent = lax.all_to_all(grad_out, "dp", split_axis=0, concat_axis=1, tiled=True)
    inputs = lax.all_gather(inputs, "expert", axis=0, tiled=True)
    cotangent = lax.all_gather(cotangent, "expert", axis=0, tiled=True)
    scaled = (cotangent.astype(jnp.float32) * weight).astype(jnp.bfloat16)
    full_gate = lax.all_gather(w_gate, "dp", axis=1, tiled=True)[0]
    full_up = lax.all_gather(w_up, "dp", axis=1, tiled=True)[0]
    full_down = lax.all_gather(w_down, "dp", axis=2, tiled=True)[0]
    pre_gate = jnp.dot(inputs, full_gate, preferred_element_type=jnp.float32)
    pre_up = jnp.dot(inputs, full_up, preferred_element_type=jnp.float32)
    sigmoid_gate = jax.nn.sigmoid(pre_gate)
    activated = pre_gate * sigmoid_gate
    hidden = (activated * pre_up).astype(jnp.bfloat16)
    back_hidden = contract_cols(scaled, full_down)
    d_up = (back_hidden * activated).astype(jnp.bfloat16)
    d_gate = (back_hidden * pre_up * sigmoid_gate * (1.0 + pre_gate * (1.0 - sigmoid_gate))).astype(
        jnp.bfloat16
    )
    row_grad = (contract_cols(d_gate, full_gate) + contract_cols(d_up, full_up)).astype(
        jnp.bfloat16
    )
    summed = lax.psum_scatter(row_grad, "expert", scatter_dimension=0, tiled=True)
    d_tokens = lax.all_to_all(summed, "dp", split_axis=1, concat_axis=0, tiled=True)
    gate_part = contract_rows(inputs, d_gate).astype(jnp.bfloat16)
    up_part = contract_rows(inputs, d_up).astype(jnp.bfloat16)
    down_part = contract_rows(hidden, scaled).astype(jnp.bfloat16)
    grad_gate = lax.psum_scatter(gate_part, "dp", scatter_dimension=0, tiled=True)
    grad_up = lax.psum_scatter(up_part, "dp", scatter_dimension=0, tiled=True)
    grad_down = lax.psum_scatter(down_part, "dp", scatter_dimension=1, tiled=True)
    return (d_tokens, grad_gate[None], grad_up[None], grad_down[None])


def solution(mesh):
    small = mesh.shape["expert"] == 16 and mesh.shape["dp"] == 2
    return jax.shard_map(
        dense_shards if small else shards,
        mesh=mesh,
        in_specs=(
            P("expert", "dp"),
            P("expert", "dp"),
            P("expert", None),
            P("expert", None),
            P("expert", "dp", None),
            P("expert", "dp", None),
            P("expert", None, "dp"),
        ),
        out_specs=(
            P("expert", "dp"),
            P("expert", "dp", None),
            P("expert", "dp", None),
            P("expert", None, "dp"),
        ),
        check_vma=False,
    )
```

```python
import jax
import jax.numpy as jnp
from jax import lax
from jax.experimental import pallas as pl
from jax.experimental.pallas import tpu as pltpu
from jax.sharding import PartitionSpec as P


def contract_rows(left_rows, right_rows):
    return lax.dot_general(
        left_rows, right_rows, (((0,), (0,)), ((), ())), preferred_element_type=jnp.float32
    )


def contract_cols(left_rows, right_rows):
    return lax.dot_general(
        left_rows, right_rows, (((1,), (1,)), ((), ())), preferred_element_type=jnp.float32
    )


def per_source(left_rows, right_rows, dp_count):
    left_split = left_rows.reshape(dp_count, -1, left_rows.shape[1])
    right_split = right_rows.reshape(dp_count, -1, right_rows.shape[1])
    partial_value = jnp.einsum(
        "jra,jrb->jab", left_split, right_split, preferred_element_type=jnp.float32
    )
    rounded = lax.optimization_barrier(partial_value.astype(jnp.bfloat16))
    return jnp.sum(rounded.astype(jnp.float32), axis=0).astype(jnp.bfloat16)


def shards(tokens, grad_out, routes, gates, w_gate, w_up, w_down):
    experts = lax.axis_size("expert")
    dp_count = lax.axis_size("dp")
    tok_count = tokens.shape[0]
    top_count = routes.shape[1]
    slot_cap = min(tok_count, max(2, 3 * tok_count * top_count // (2 * experts)))
    row_total = tok_count * top_count
    flat_routes = routes.reshape(-1)
    flat_gates = gates.reshape(-1)
    onehot = (flat_routes[:, None] == jnp.arange(experts, dtype=jnp.int32)[None, :]).astype(
        jnp.int32
    )
    slot_rank = jnp.sum((jnp.cumsum(onehot, axis=0) - onehot) * onehot, axis=1)
    slot_index = flat_routes * slot_cap + slot_rank
    slot_source = (
        jnp.full((experts * slot_cap,), row_total, jnp.int32)
        .at[slot_index]
        .set(jnp.arange(row_total, dtype=jnp.int32))
    )
    valid = slot_source < row_total
    safe_rows = jnp.where(valid, slot_source, 0)
    token_ids = safe_rows // top_count
    token_slots = jnp.where(valid[:, None], tokens[token_ids], jnp.zeros((), tokens.dtype))
    scaled_slots = jnp.where(
        valid[:, None],
        grad_out[token_ids].astype(jnp.float32) * flat_gates[safe_rows][:, None],
        0.0,
    ).astype(jnp.bfloat16)
    input_cols, scaled_cols = (
        lax.all_to_all(token_slots, "expert", split_axis=0, concat_axis=0, tiled=True),
        lax.all_to_all(scaled_slots, "expert", split_axis=0, concat_axis=0, tiled=True),
    )
    inputs, scaled = (
        lax.all_to_all(input_cols, "dp", split_axis=0, concat_axis=1, tiled=True),
        lax.all_to_all(scaled_cols, "dp", split_axis=0, concat_axis=1, tiled=True),
    )
    full_gate, full_up, full_down = (
        lax.all_gather(w_gate, "dp", axis=1, tiled=True),
        lax.all_gather(w_up, "dp", axis=1, tiled=True),
        lax.all_gather(w_down, "dp", axis=2, tiled=True),
    )
    full_gate = full_gate[0]
    full_up = full_up[0]
    full_down = full_down[0]
    pre_gate = jnp.dot(inputs, full_gate, preferred_element_type=jnp.float32)
    pre_up = jnp.dot(inputs, full_up, preferred_element_type=jnp.float32)
    sigmoid_gate = jax.nn.sigmoid(pre_gate)
    activated = pre_gate * sigmoid_gate
    hidden = (activated * pre_up).astype(jnp.bfloat16)
    back_hidden = contract_cols(scaled, full_down)
    d_up = (back_hidden * activated).astype(jnp.bfloat16)
    d_gate = (back_hidden * pre_up * sigmoid_gate * (1.0 + pre_gate * (1.0 - sigmoid_gate))).astype(
        jnp.bfloat16
    )
    row_grad = (contract_cols(d_gate, full_gate) + contract_cols(d_up, full_up)).astype(
        jnp.bfloat16
    )
    came_back = lax.all_to_all(
        lax.all_to_all(row_grad, "dp", split_axis=1, concat_axis=0, tiled=True),
        "expert",
        split_axis=0,
        concat_axis=0,
        tiled=True,
    )
    picked = came_back[slot_index].astype(jnp.float32)
    d_tokens = jnp.sum(picked.reshape(tok_count, top_count, -1), axis=1).astype(jnp.bfloat16)
    hidden_all = lax.all_gather(hidden, "dp", axis=0, tiled=True)
    grad_down = per_source(hidden_all, scaled_cols, dp_count)
    gate_part = contract_rows(inputs, d_gate).astype(jnp.bfloat16).astype(jnp.float32)
    up_part = contract_rows(inputs, d_up).astype(jnp.bfloat16).astype(jnp.float32)
    gate_sum, up_sum = (
        lax.psum_scatter(
            gate_part.astype(jnp.bfloat16), "dp", scatter_dimension=0, tiled=True
        ).astype(jnp.float32),
        lax.psum_scatter(
            up_part.astype(jnp.bfloat16), "dp", scatter_dimension=0, tiled=True
        ).astype(jnp.float32),
    )
    grad_gate = gate_sum.astype(jnp.bfloat16)
    grad_up = up_sum.astype(jnp.bfloat16)
    return (d_tokens, grad_gate[None], grad_up[None], grad_down[None])


MESH_ID = pl.DeviceIdType.MESH


def contract_first(left, right):
    return lax.dot_general(left, right, (((0,), (0,)), ((), ())), preferred_element_type=jnp.float32)


def fused_kernel(
    tok, cot, tab, wg, wu, wd,
    out_tok, out_gate, out_up, out_down,
    acts, table, w_own, w_far, wd_far, scaled, pre, hidden, d_both,
    row_grad, from_core, from_y, from_z, tok_send, tok_far,
    gate_own, down_own, gate_send, up_send, down_send, gate_far, up_far, down_far,
    x_send, x_recv, z_send, z_recv, y_send, y_recv, c_send, c_recv,
    rc_send, rc_recv, ry_send, ry_recv, rz_send, rz_recv,
):
    e = lax.axis_index("expert")
    d = lax.axis_index("dp")
    core = e % 2
    y_pos = (e // 2) % 2
    z_pos = e // 4
    half = tok.shape[0] // 2
    feats = tok.shape[1]
    width = wg.shape[1]
    x_peer = (e, 1 - d)
    core_peer = (e + 1 - 2 * core, d)
    y_peer = (e + 2 - 4 * y_pos, d)
    z_peers = [((z_pos + k) % 4 * 4 + e % 4, d) for k in (1, 2, 3)]

    def copy(src, dst, send, recv, peer):
        return pltpu.make_async_remote_copy(
            src_ref=src, dst_ref=dst, send_sem=send, recv_sem=recv, device_id=peer, device_id_type=MESH_ID
        )

    barrier = pltpu.get_barrier_semaphore()
    for peer in [x_peer, core_peer, y_peer] + z_peers:
        pl.semaphore_signal(barrier, inc=1, device_id=peer, device_id_type=MESH_ID)

    mine = pl.ds(pl.multiple_of(d * half, half), half)
    theirs = pl.ds(pl.multiple_of((1 - d) * half, half), half)
    acts[0, 0, 0] = tok[mine, :]
    acts[0, 0, 1] = cot[mine, :]
    table[0] = tab[mine, :]
    pl.semaphore_wait(barrier, 6)

    sends = []

    def start(item):
        item.start()
        sends.append(item)
        return item

    swap_tok = start(copy(tok.at[theirs], acts.at[1, 0, 0], x_send.at[0], x_recv.at[0], x_peer))
    swap_cot = start(copy(cot.at[theirs], acts.at[1, 0, 1], x_send.at[1], x_recv.at[1], x_peer))

    pieces = [acts.at[0], acts.at[1], table]

    def z_copy(p, k):
        return copy(pieces[p].at[0], pieces[p].at[4 - k], z_send.at[p, k - 1], z_recv.at[p, 3 - k], z_peers[k - 1])

    def y_copy(p, j):
        return copy(pieces[p].at[j], pieces[p].at[4 + j], y_send.at[p, j], y_recv.at[p, j], y_peer)

    def c_copy(p, j):
        return copy(pieces[p].at[j], pieces[p].at[8 + j], c_send.at[p, j], c_recv.at[p, j], core_peer)

    def spread_own(p):
        for k in (2, 1, 3):
            start(z_copy(p, k))
        start(y_copy(p, 0))
        start(c_copy(p, 0))

    def forward(p):
        for j in (1, 3, 2):
            z_copy(p, 4 - j).wait_recv()
            start(y_copy(p, j))
            start(c_copy(p, j))
        for j in (0, 1, 3, 2):
            y_copy(p, j).wait_recv()
            start(c_copy(p, 4 + j))

    spread_own(2)
    spread_own(0)
    swap_tok.wait_recv()
    swap_cot.wait_recv()
    spread_own(1)
    w_copies = [
        start(copy(wg, w_far.at[:, pl.ds(0, width)], x_send.at[2], x_recv.at[2], x_peer)),
        start(copy(wu, w_far.at[:, pl.ds(width, width)], x_send.at[3], x_recv.at[3], x_peer)),
    ]
    w_own[:, :width] = wg[...]
    w_own[:, width:] = wu[...]
    forward(2)
    forward(0)
    down_copy = start(copy(wd, wd_far, x_send.at[4], x_recv.at[4], x_peer))
    forward(1)
    for p in (2, 0, 1):
        for j in range(8):
            c_copy(p, j).wait_recv()
    for item in w_copies:
        item.wait_recv()

    tile = 4 * half
    blocks = 4

    def rows_of(i):
        return pl.ds(pl.multiple_of(i * tile, tile), tile)

    @pl.loop(0, blocks)
    def _(i):
        rows, group = rows_of(i), pl.ds(i * 4, 4)
        lanes = lax.broadcasted_iota(jnp.int32, (tile, table.shape[-1]), 1)
        column = jnp.sum(
            jnp.where(lanes == e, table[group].reshape(tile, -1), 0.0), axis=1, keepdims=True
        )
        for h in range(2):
            far = acts[h, group, 1].reshape(tile, feats).astype(jnp.float32)
            scaled[h, rows, :] = (far * column).astype(jnp.bfloat16)
        near = jnp.dot(acts[0, group, 0].reshape(tile, feats), w_own[...], preferred_element_type=jnp.float32)
        far = jnp.dot(acts[1, group, 0].reshape(tile, feats), w_far[...], preferred_element_type=jnp.float32)
        total = near + far
        pre[rows, :] = total
        gate, up = total[:, :width], total[:, width:]
        hidden[rows, :] = (gate * jax.nn.sigmoid(gate) * up).astype(jnp.bfloat16)

    strip = feats // 4

    def cols_of(i):
        return pl.ds(pl.multiple_of(i * strip, strip), strip)

    @pl.loop(0, 4)
    def _(i):
        down_send[:, cols_of(i)] = contract_first(hidden[...], scaled[1, :, cols_of(i)]).astype(jnp.bfloat16)

    grad_copies = [start(copy(down_send, down_far, x_send.at[5], x_recv.at[5], x_peer))]
    down_copy.wait_recv()

    @pl.loop(0, blocks)
    def _(i):
        rows = rows_of(i)
        back = contract_cols(scaled[0, rows, :], wd[...]) + contract_cols(scaled[1, rows, :], wd_far[...])
        gate, up = pre[rows, :width], pre[rows, width:]
        sig = jax.nn.sigmoid(gate)
        d_both[rows, :width] = (back * up * sig * (1.0 + gate * (1.0 - sig))).astype(jnp.bfloat16)
        d_both[rows, width:] = (back * (gate * sig)).astype(jnp.bfloat16)

    def rc_copy(h):
        return copy(row_grad.at[h, pl.ds(8, 8)], from_core.at[h], rc_send.at[h], rc_recv.at[h], core_peer)

    def ry_copy(h):
        return copy(row_grad.at[h, pl.ds(4, 4)], from_y.at[h], ry_send.at[h], ry_recv.at[h], y_peer)

    def rz_copy(h, k):
        return copy(row_grad.at[h, k], from_z.at[h, 3 - k], rz_send.at[h, k - 1], rz_recv.at[h, 3 - k], z_peers[k - 1])

    def rows_back(h, first):
        weights = w_own if h == 0 else w_far

        @pl.loop(first, first + 2)
        def _(i):
            value = contract_cols(d_both[rows_of(i), :], weights[...])
            row_grad[h, pl.ds(i * 4, 4)] = value.astype(jnp.bfloat16).reshape(4, half, feats)

    def add_into(h, first, extra, offset):
        @pl.loop(0, 4)
        def _(j):
            near = row_grad[h, first + j].astype(jnp.float32)
            row_grad[h, first + j] = (near + extra[h, offset + j].astype(jnp.float32)).astype(jnp.bfloat16)

    rows_back(1, 2)
    start(rc_copy(1))

    @pl.loop(0, 4)
    def _(i):
        left = acts[1, :, 0, :, cols_of(i)].reshape(16 * half, strip)
        value = contract_first(left, d_both[...]).astype(jnp.bfloat16)
        gate_send[cols_of(i), :] = value[:, :width]
        up_send[cols_of(i), :] = value[:, width:]

    grad_copies.append(start(copy(gate_send, gate_far, x_send.at[6], x_recv.at[6], x_peer)))
    grad_copies.append(start(copy(up_send, up_far, x_send.at[7], x_recv.at[7], x_peer)))

    rows_back(1, 0)
    rc_copy(1).wait_recv()
    add_into(1, 4, from_core, 4)
    start(ry_copy(1))
    rows_back(0, 2)
    start(rc_copy(0))
    rows_back(0, 0)
    add_into(1, 0, from_core, 0)
    rc_copy(0).wait_recv()
    add_into(0, 4, from_core, 4)
    start(ry_copy(0))
    add_into(0, 0, from_core, 0)

    ry_copy(1).wait_recv()
    add_into(1, 0, from_y, 0)
    for k in (2, 1, 3):
        start(rz_copy(1, k))

    @pl.loop(0, 4)
    def _(i):
        left = acts[0, :, 0, :, cols_of(i)].reshape(16 * half, strip)
        gate_own[cols_of(i), :] = contract_first(left, d_both[...])
        down_own[:, cols_of(i)] = contract_first(hidden[...], scaled[0, :, cols_of(i)])

    ry_copy(0).wait_recv()
    add_into(0, 0, from_y, 0)
    for k in (2, 1, 3):
        start(rz_copy(0, k))

    def finish(h):
        total = row_grad[h, 0].astype(jnp.float32)
        for k in range(3):
            rz_copy(h, 3 - k).wait_recv()
        for k in range(3):
            total = total + from_z[h, k].astype(jnp.float32)
        return total.astype(jnp.bfloat16)

    tok_send[...] = finish(1)
    tok_copy = start(copy(tok_send, tok_far, x_send.at[8], x_recv.at[8], x_peer))
    out_tok[mine, :] = finish(0)

    grad_copies[0].wait_recv()
    out_down[...] = (down_own[...] + down_far[...].astype(jnp.float32)).astype(jnp.bfloat16)
    grad_copies[1].wait_recv()
    out_gate[...] = (gate_own[:, :width] + gate_far[...].astype(jnp.float32)).astype(jnp.bfloat16)
    grad_copies[2].wait_recv()
    out_up[...] = (gate_own[:, width:] + up_far[...].astype(jnp.float32)).astype(jnp.bfloat16)
    tok_copy.wait_recv()
    out_tok[theirs, :] = tok_far[...]
    for item in sends:
        item.wait_send()


def dense_shards(tokens, grad_out, routes, gates, w_gate, w_up, w_down):
    experts = lax.axis_size("expert")
    tok_count, feats = tokens.shape
    width = w_gate.shape[2]
    half = tok_count // 2
    named = routes[:, :, None] == jnp.arange(128, dtype=jnp.int32)
    table = jnp.sum(jnp.where(named, gates[:, :, None], 0.0), axis=1)
    bf, f32 = jnp.bfloat16, jnp.float32
    rows = experts * half
    vmem = pl.BlockSpec(memory_space=pltpu.VMEM)
    dma = pltpu.SemaphoreType.DMA
    d_tokens, grad_gate, grad_up, grad_down = pl.pallas_call(
        fused_kernel,
        out_shape=(
            jax.ShapeDtypeStruct((tok_count, feats), bf),
            jax.ShapeDtypeStruct((feats, width), bf),
            jax.ShapeDtypeStruct((feats, width), bf),
            jax.ShapeDtypeStruct((width, feats), bf),
        ),
        in_specs=[vmem] * 6,
        out_specs=(vmem,) * 4,
        scratch_shapes=[
            pltpu.VMEM((2, experts, 2, half, feats), bf),
            pltpu.VMEM((experts, half, 128), f32),
            pltpu.VMEM((feats, 2 * width), bf),
            pltpu.VMEM((feats, 2 * width), bf),
            pltpu.VMEM((width, feats), bf),
            pltpu.VMEM((2, rows, feats), bf),
            pltpu.VMEM((rows, 2 * width), f32),
            pltpu.VMEM((rows, width), bf),
            pltpu.VMEM((rows, 2 * width), bf),
            pltpu.VMEM((2, experts, half, feats), bf),
            pltpu.VMEM((2, 8, half, feats), bf),
            pltpu.VMEM((2, 4, half, feats), bf),
            pltpu.VMEM((2, 3, half, feats), bf),
            pltpu.VMEM((half, feats), bf),
            pltpu.VMEM((half, feats), bf),
            pltpu.VMEM((feats, 2 * width), f32),
            pltpu.VMEM((width, feats), f32),
            pltpu.VMEM((feats, width), bf),
            pltpu.VMEM((feats, width), bf),
            pltpu.VMEM((width, feats), bf),
            pltpu.VMEM((feats, width), bf),
            pltpu.VMEM((feats, width), bf),
            pltpu.VMEM((width, feats), bf),
            dma((9,)), dma((9,)),
            dma((3, 3)), dma((3, 3)),
            dma((3, 4)), dma((3, 4)),
            dma((3, 8)), dma((3, 8)),
            dma((2,)), dma((2,)),
            dma((2,)), dma((2,)),
            dma((2, 3)), dma((2, 3)),
        ],
        compiler_params=pltpu.CompilerParams(
            collective_id=0, has_side_effects=True, vmem_limit_bytes=60 * 1024 * 1024
        ),
        cost_estimate=pl.CostEstimate(
            flops=16 * rows * 2 * feats * width, bytes_accessed=8 * 1024 * 1024, transcendentals=rows * width
        ),
    )(tokens, grad_out, table, w_gate[0], w_up[0], w_down[0])
    return (d_tokens, grad_gate[None], grad_up[None], grad_down[None])


def solution(mesh):
    small = mesh.shape["expert"] == 16 and mesh.shape["dp"] == 2
    return jax.shard_map(
        dense_shards if small else shards,
        mesh=mesh,
        in_specs=(
            P("expert", "dp"),
            P("expert", "dp"),
            P("expert", None),
            P("expert", None),
            P("expert", "dp", None),
            P("expert", "dp", None),
            P("expert", None, "dp"),
        ),
        out_specs=(
            P("expert", "dp"),
            P("expert", "dp", None),
            P("expert", "dp", None),
            P("expert", None, "dp"),
        ),
        check_vma=False,
    )
```

```python
import jax
import jax.numpy as jnp
from jax import lax
from jax.experimental import pallas as pl
from jax.experimental.pallas import tpu as pltpu
from jax.sharding import PartitionSpec as P


def contract_rows(left_rows, right_rows):
    return lax.dot_general(
        left_rows, right_rows, (((0,), (0,)), ((), ())), preferred_element_type=jnp.float32
    )


def contract_cols(left_rows, right_rows):
    return lax.dot_general(
        left_rows, right_rows, (((1,), (1,)), ((), ())), preferred_element_type=jnp.float32
    )


def per_source(left_rows, right_rows, dp_count):
    left_split = left_rows.reshape(dp_count, -1, left_rows.shape[1])
    right_split = right_rows.reshape(dp_count, -1, right_rows.shape[1])
    partial_value = jnp.einsum(
        "jra,jrb->jab", left_split, right_split, preferred_element_type=jnp.float32
    )
    rounded = lax.optimization_barrier(partial_value.astype(jnp.bfloat16))
    return jnp.sum(rounded.astype(jnp.float32), axis=0).astype(jnp.bfloat16)


def shards(tokens, grad_out, routes, gates, w_gate, w_up, w_down):
    experts = lax.axis_size("expert")
    dp_count = lax.axis_size("dp")
    tok_count = tokens.shape[0]
    top_count = routes.shape[1]
    slot_cap = min(tok_count, max(2, 3 * tok_count * top_count // (2 * experts)))
    row_total = tok_count * top_count
    flat_routes = routes.reshape(-1)
    flat_gates = gates.reshape(-1)
    onehot = (flat_routes[:, None] == jnp.arange(experts, dtype=jnp.int32)[None, :]).astype(
        jnp.int32
    )
    slot_rank = jnp.sum((jnp.cumsum(onehot, axis=0) - onehot) * onehot, axis=1)
    slot_index = flat_routes * slot_cap + slot_rank
    slot_source = (
        jnp.full((experts * slot_cap,), row_total, jnp.int32)
        .at[slot_index]
        .set(jnp.arange(row_total, dtype=jnp.int32))
    )
    valid = slot_source < row_total
    safe_rows = jnp.where(valid, slot_source, 0)
    token_ids = safe_rows // top_count
    token_slots = jnp.where(valid[:, None], tokens[token_ids], jnp.zeros((), tokens.dtype))
    scaled_slots = jnp.where(
        valid[:, None],
        grad_out[token_ids].astype(jnp.float32) * flat_gates[safe_rows][:, None],
        0.0,
    ).astype(jnp.bfloat16)
    input_cols, scaled_cols = (
        lax.all_to_all(token_slots, "expert", split_axis=0, concat_axis=0, tiled=True),
        lax.all_to_all(scaled_slots, "expert", split_axis=0, concat_axis=0, tiled=True),
    )
    inputs, scaled = (
        lax.all_to_all(input_cols, "dp", split_axis=0, concat_axis=1, tiled=True),
        lax.all_to_all(scaled_cols, "dp", split_axis=0, concat_axis=1, tiled=True),
    )
    full_gate, full_up, full_down = (
        lax.all_gather(w_gate, "dp", axis=1, tiled=True),
        lax.all_gather(w_up, "dp", axis=1, tiled=True),
        lax.all_gather(w_down, "dp", axis=2, tiled=True),
    )
    full_gate = full_gate[0]
    full_up = full_up[0]
    full_down = full_down[0]
    pre_gate = jnp.dot(inputs, full_gate, preferred_element_type=jnp.float32)
    pre_up = jnp.dot(inputs, full_up, preferred_element_type=jnp.float32)
    sigmoid_gate = jax.nn.sigmoid(pre_gate)
    activated = pre_gate * sigmoid_gate
    hidden = (activated * pre_up).astype(jnp.bfloat16)
    back_hidden = contract_cols(scaled, full_down)
    d_up = (back_hidden * activated).astype(jnp.bfloat16)
    d_gate = (back_hidden * pre_up * sigmoid_gate * (1.0 + pre_gate * (1.0 - sigmoid_gate))).astype(
        jnp.bfloat16
    )
    row_grad = (contract_cols(d_gate, full_gate) + contract_cols(d_up, full_up)).astype(
        jnp.bfloat16
    )
    came_back = lax.all_to_all(
        lax.all_to_all(row_grad, "dp", split_axis=1, concat_axis=0, tiled=True),
        "expert",
        split_axis=0,
        concat_axis=0,
        tiled=True,
    )
    picked = came_back[slot_index].astype(jnp.float32)
    d_tokens = jnp.sum(picked.reshape(tok_count, top_count, -1), axis=1).astype(jnp.bfloat16)
    hidden_all = lax.all_gather(hidden, "dp", axis=0, tiled=True)
    grad_down = per_source(hidden_all, scaled_cols, dp_count)
    gate_part = contract_rows(inputs, d_gate).astype(jnp.bfloat16).astype(jnp.float32)
    up_part = contract_rows(inputs, d_up).astype(jnp.bfloat16).astype(jnp.float32)
    gate_sum, up_sum = (
        lax.psum_scatter(
            gate_part.astype(jnp.bfloat16), "dp", scatter_dimension=0, tiled=True
        ).astype(jnp.float32),
        lax.psum_scatter(
            up_part.astype(jnp.bfloat16), "dp", scatter_dimension=0, tiled=True
        ).astype(jnp.float32),
    )
    grad_gate = gate_sum.astype(jnp.bfloat16)
    grad_up = up_sum.astype(jnp.bfloat16)
    return (d_tokens, grad_gate[None], grad_up[None], grad_down[None])


MESH_ID = pl.DeviceIdType.MESH


def contract_first(left, right):
    return lax.dot_general(left, right, (((0,), (0,)), ((), ())), preferred_element_type=jnp.float32)


def fused_kernel(
    tok, cot, tab, wg, wu, wd,
    out_tok, out_gate, out_up, out_down,
    acts, table, w_own, w_far, wd_far, scaled, pre, hidden, d_both,
    row_grad, from_core, from_y, from_z, tok_send, tok_far,
    gate_own, down_own, gate_send, up_send, down_send, gate_far, up_far, down_far,
    x_send, x_recv, z_send, z_recv, y_send, y_recv, c_send, c_recv,
    rc_send, rc_recv, ry_send, ry_recv, rz_send, rz_recv,
):
    e = lax.axis_index("expert")
    d = lax.axis_index("dp")
    core = e % 2
    y_pos = (e // 2) % 2
    z_pos = e // 4
    half = tok.shape[0] // 2
    feats = tok.shape[1]
    width = wg.shape[1]
    x_peer = (e, 1 - d)
    core_peer = (e + 1 - 2 * core, d)
    y_peer = (e + 2 - 4 * y_pos, d)
    z_peers = [((z_pos + k) % 4 * 4 + e % 4, d) for k in (1, 2, 3)]

    def copy(src, dst, send, recv, peer):
        return pltpu.make_async_remote_copy(
            src_ref=src, dst_ref=dst, send_sem=send, recv_sem=recv, device_id=peer, device_id_type=MESH_ID
        )

    barrier = pltpu.get_barrier_semaphore()
    for peer in [x_peer, core_peer, y_peer] + z_peers:
        pl.semaphore_signal(barrier, inc=1, device_id=peer, device_id_type=MESH_ID)

    mine = pl.ds(pl.multiple_of(d * half, half), half)
    theirs = pl.ds(pl.multiple_of((1 - d) * half, half), half)
    acts[0, 0, 0] = tok[mine, :]
    acts[0, 0, 1] = cot[mine, :]
    table[0] = tab[mine, :]
    pl.semaphore_wait(barrier, 6)

    sends = []

    def start(item):
        item.start()
        sends.append(item)
        return item

    swap_tok = start(copy(tok.at[theirs], acts.at[1, 0, 0], x_send.at[0], x_recv.at[0], x_peer))
    swap_cot = start(copy(cot.at[theirs], acts.at[1, 0, 1], x_send.at[1], x_recv.at[1], x_peer))

    pieces = [acts.at[0], acts.at[1], table]
    up_peer = ((z_pos + 1) % 4 * 4 + e % 4, d)
    down_peer = ((z_pos + 3) % 4 * 4 + e % 4, d)
    guarded = []

    def line_copy(p, base, src, dst, send, peer):
        return copy(
            pieces[p].at[base + src],
            pieces[p].at[base + dst],
            z_send.at[p, base // 4, send],
            z_recv.at[p, base // 4, dst - 1],
            peer,
        )

    def start_when(condition, item):
        pl.when(condition)(item.start)
        guarded.append((condition, item))

    def line_start(p, base):
        start_when(z_pos < 3, line_copy(p, base, 0, 3, 0, up_peer))
        start_when(z_pos > 0, line_copy(p, base, 0, 1, 1, down_peer))

    def line_step(p, base, j):
        line_copy(p, base, 0, j, 0, up_peer).wait_recv()
        if j == 1:
            start_when((z_pos > 0) & (z_pos < 3), line_copy(p, base, 1, 2, 2, down_peer))
        elif j == 3:
            start_when((z_pos > 0) & (z_pos < 3), line_copy(p, base, 3, 2, 3, up_peer))
        else:
            start_when(z_pos == 1, line_copy(p, base, 2, 3, 4, down_peer))
            start_when(z_pos == 2, line_copy(p, base, 2, 1, 4, up_peer))

    def y_copy(p, j):
        return copy(pieces[p].at[j], pieces[p].at[4 + j], y_send.at[p, j], y_recv.at[p, j], y_peer)

    def c_copy(p, j):
        return copy(pieces[p].at[j], pieces[p].at[8 + j], c_send.at[p, j], c_recv.at[p, j], core_peer)

    for p in (2, 0):
        line_start(p, 0)
        start(y_copy(p, 0))
        start(c_copy(p, 0))
    w_own[:, :width] = wg[...]
    w_own[:, width:] = wu[...]
    swap_tok.wait_recv()
    swap_cot.wait_recv()
    start(y_copy(1, 0))
    line_start(1, 0)
    start(c_copy(1, 0))
    w_copies = [
        start(copy(wg, w_far.at[:, pl.ds(0, width)], x_send.at[2], x_recv.at[2], x_peer)),
        start(copy(wu, w_far.at[:, pl.ds(width, width)], x_send.at[3], x_recv.at[3], x_peer)),
    ]
    down_copy = start(copy(wd, wd_far, x_send.at[4], x_recv.at[4], x_peer))
    for j in (1, 3, 2):
        for p in (2, 0):
            line_step(p, 0, j)
            start(y_copy(p, j))
            start(c_copy(p, j))
        if j == 3:
            y_copy(1, 0).wait_recv()
            line_start(1, 4)
            start(c_copy(1, 4))
    for j in (1, 3, 2):
        for base in (0, 4):
            line_step(1, base, j)
            start(c_copy(1, base + j))
    for j in (0, 1, 3, 2):
        for p in (2, 0):
            y_copy(p, j).wait_recv()
            start(c_copy(p, 4 + j))
    for p in (2, 0, 1):
        for j in range(8):
            c_copy(p, j).wait_recv()
    for item in w_copies:
        item.wait_recv()

    tile = 4 * half
    blocks = 4

    def rows_of(i):
        return pl.ds(pl.multiple_of(i * tile, tile), tile)

    @pl.loop(0, blocks)
    def _(i):
        rows, group = rows_of(i), pl.ds(i * 4, 4)
        lanes = lax.broadcasted_iota(jnp.int32, (tile, table.shape[-1]), 1)
        column = jnp.sum(
            jnp.where(lanes == e, table[group].reshape(tile, -1), 0.0), axis=1, keepdims=True
        )
        for h in range(2):
            far = acts[h, group, 1].reshape(tile, feats).astype(jnp.float32)
            scaled[h, rows, :] = (far * column).astype(jnp.bfloat16)
        near = jnp.dot(acts[0, group, 0].reshape(tile, feats), w_own[...], preferred_element_type=jnp.float32)
        far = jnp.dot(acts[1, group, 0].reshape(tile, feats), w_far[...], preferred_element_type=jnp.float32)
        total = near + far
        pre[rows, :] = total
        gate, up = total[:, :width], total[:, width:]
        hidden[rows, :] = (gate * jax.nn.sigmoid(gate) * up).astype(jnp.bfloat16)

    strip = feats // 4

    def cols_of(i):
        return pl.ds(pl.multiple_of(i * strip, strip), strip)

    @pl.loop(0, 4)
    def _(i):
        down_send[:, cols_of(i)] = contract_first(hidden[...], scaled[1, :, cols_of(i)]).astype(jnp.bfloat16)

    grad_copies = [start(copy(down_send, down_far, x_send.at[5], x_recv.at[5], x_peer))]
    down_copy.wait_recv()

    @pl.loop(0, blocks)
    def _(i):
        rows = rows_of(i)
        back = contract_cols(scaled[0, rows, :], wd[...]) + contract_cols(scaled[1, rows, :], wd_far[...])
        gate, up = pre[rows, :width], pre[rows, width:]
        sig = jax.nn.sigmoid(gate)
        d_both[rows, :width] = (back * up * sig * (1.0 + gate * (1.0 - sig))).astype(jnp.bfloat16)
        d_both[rows, width:] = (back * (gate * sig)).astype(jnp.bfloat16)

    def rc_copy(h):
        return copy(row_grad.at[h, pl.ds(8, 8)], from_core.at[h], rc_send.at[h], rc_recv.at[h], core_peer)

    def ry_copy(h):
        return copy(row_grad.at[h, pl.ds(4, 4)], from_y.at[h], ry_send.at[h], ry_recv.at[h], y_peer)

    def rz_copy(h, k):
        return copy(row_grad.at[h, k], from_z.at[h, 3 - k], rz_send.at[h, k - 1], rz_recv.at[h, 3 - k], z_peers[k - 1])

    def rows_back(h, first):
        weights = w_own if h == 0 else w_far

        @pl.loop(first, first + 2)
        def _(i):
            value = contract_cols(d_both[rows_of(i), :], weights[...])
            row_grad[h, pl.ds(i * 4, 4)] = value.astype(jnp.bfloat16).reshape(4, half, feats)

    def add_into(h, first, extra, offset):
        @pl.loop(0, 4)
        def _(j):
            near = row_grad[h, first + j].astype(jnp.float32)
            row_grad[h, first + j] = (near + extra[h, offset + j].astype(jnp.float32)).astype(jnp.bfloat16)

    rows_back(1, 2)
    start(rc_copy(1))
    rows_back(0, 2)
    start(rc_copy(0))
    rows_back(1, 0)
    rc_copy(1).wait_recv()
    add_into(1, 4, from_core, 4)
    start(ry_copy(1))

    @pl.loop(0, 4)
    def _(i):
        left = acts[1, :, 0, :, cols_of(i)].reshape(16 * half, strip)
        value = contract_first(left, d_both[...]).astype(jnp.bfloat16)
        gate_send[cols_of(i), :] = value[:, :width]
        up_send[cols_of(i), :] = value[:, width:]

    grad_copies.append(start(copy(gate_send, gate_far, x_send.at[6], x_recv.at[6], x_peer)))
    grad_copies.append(start(copy(up_send, up_far, x_send.at[7], x_recv.at[7], x_peer)))

    rows_back(0, 0)
    rc_copy(0).wait_recv()
    add_into(0, 4, from_core, 4)
    start(ry_copy(0))
    add_into(1, 0, from_core, 0)
    add_into(0, 0, from_core, 0)

    ry_copy(1).wait_recv()
    add_into(1, 0, from_y, 0)
    for k in (2, 1, 3):
        start(rz_copy(1, k))

    @pl.loop(0, 4)
    def _(i):
        left = acts[0, :, 0, :, cols_of(i)].reshape(16 * half, strip)
        gate_own[cols_of(i), :] = contract_first(left, d_both[...])
        down_own[:, cols_of(i)] = contract_first(hidden[...], scaled[0, :, cols_of(i)])

    ry_copy(0).wait_recv()
    add_into(0, 0, from_y, 0)
    for k in (2, 1, 3):
        start(rz_copy(0, k))

    def finish(h):
        total = row_grad[h, 0].astype(jnp.float32)
        for k in range(3):
            rz_copy(h, 3 - k).wait_recv()
        for k in range(3):
            total = total + from_z[h, k].astype(jnp.float32)
        return total.astype(jnp.bfloat16)

    tok_send[...] = finish(1)
    tok_copy = start(copy(tok_send, tok_far, x_send.at[8], x_recv.at[8], x_peer))
    out_tok[mine, :] = finish(0)

    grad_copies[0].wait_recv()
    out_down[...] = (down_own[...] + down_far[...].astype(jnp.float32)).astype(jnp.bfloat16)
    grad_copies[1].wait_recv()
    out_gate[...] = (gate_own[:, :width] + gate_far[...].astype(jnp.float32)).astype(jnp.bfloat16)
    grad_copies[2].wait_recv()
    out_up[...] = (gate_own[:, width:] + up_far[...].astype(jnp.float32)).astype(jnp.bfloat16)
    tok_copy.wait_recv()
    out_tok[theirs, :] = tok_far[...]
    for item in sends:
        item.wait_send()
    for condition, item in guarded:
        pl.when(condition)(item.wait_send)


def dense_shards(tokens, grad_out, routes, gates, w_gate, w_up, w_down):
    experts = lax.axis_size("expert")
    tok_count, feats = tokens.shape
    width = w_gate.shape[2]
    half = tok_count // 2
    named = routes[:, :, None] == jnp.arange(128, dtype=jnp.int32)
    table = jnp.sum(jnp.where(named, gates[:, :, None], 0.0), axis=1)
    bf, f32 = jnp.bfloat16, jnp.float32
    rows = experts * half
    vmem = pl.BlockSpec(memory_space=pltpu.VMEM)
    dma = pltpu.SemaphoreType.DMA
    d_tokens, grad_gate, grad_up, grad_down = pl.pallas_call(
        fused_kernel,
        out_shape=(
            jax.ShapeDtypeStruct((tok_count, feats), bf),
            jax.ShapeDtypeStruct((feats, width), bf),
            jax.ShapeDtypeStruct((feats, width), bf),
            jax.ShapeDtypeStruct((width, feats), bf),
        ),
        in_specs=[vmem] * 6,
        out_specs=(vmem,) * 4,
        scratch_shapes=[
            pltpu.VMEM((2, experts, 2, half, feats), bf),
            pltpu.VMEM((experts, half, 128), f32),
            pltpu.VMEM((feats, 2 * width), bf),
            pltpu.VMEM((feats, 2 * width), bf),
            pltpu.VMEM((width, feats), bf),
            pltpu.VMEM((2, rows, feats), bf),
            pltpu.VMEM((rows, 2 * width), f32),
            pltpu.VMEM((rows, width), bf),
            pltpu.VMEM((rows, 2 * width), bf),
            pltpu.VMEM((2, experts, half, feats), bf),
            pltpu.VMEM((2, 8, half, feats), bf),
            pltpu.VMEM((2, 4, half, feats), bf),
            pltpu.VMEM((2, 3, half, feats), bf),
            pltpu.VMEM((half, feats), bf),
            pltpu.VMEM((half, feats), bf),
            pltpu.VMEM((feats, 2 * width), f32),
            pltpu.VMEM((width, feats), f32),
            pltpu.VMEM((feats, width), bf),
            pltpu.VMEM((feats, width), bf),
            pltpu.VMEM((width, feats), bf),
            pltpu.VMEM((feats, width), bf),
            pltpu.VMEM((feats, width), bf),
            pltpu.VMEM((width, feats), bf),
            dma((9,)), dma((9,)),
            dma((3, 2, 5)), dma((3, 2, 3)),
            dma((3, 4)), dma((3, 4)),
            dma((3, 8)), dma((3, 8)),
            dma((2,)), dma((2,)),
            dma((2,)), dma((2,)),
            dma((2, 3)), dma((2, 3)),
        ],
        compiler_params=pltpu.CompilerParams(
            collective_id=0, has_side_effects=True, vmem_limit_bytes=60 * 1024 * 1024
        ),
        cost_estimate=pl.CostEstimate(
            flops=16 * rows * 2 * feats * width, bytes_accessed=8 * 1024 * 1024, transcendentals=rows * width
        ),
    )(tokens, grad_out, table, w_gate[0], w_up[0], w_down[0])
    return (d_tokens, grad_gate[None], grad_up[None], grad_down[None])


def solution(mesh):
    small = mesh.shape["expert"] == 16 and mesh.shape["dp"] == 2
    return jax.shard_map(
        dense_shards if small else shards,
        mesh=mesh,
        in_specs=(
            P("expert", "dp"),
            P("expert", "dp"),
            P("expert", None),
            P("expert", None),
            P("expert", "dp", None),
            P("expert", "dp", None),
            P("expert", None, "dp"),
        ),
        out_specs=(
            P("expert", "dp"),
            P("expert", "dp", None),
            P("expert", "dp", None),
            P("expert", None, "dp"),
        ),
        check_vma=False,
    )
```

```python
import jax
import jax.numpy as jnp
from jax import lax
from jax.experimental import pallas as pl
from jax.experimental.pallas import tpu as pltpu
from jax.sharding import PartitionSpec as P


def contract_rows(left_rows, right_rows):
    return lax.dot_general(
        left_rows, right_rows, (((0,), (0,)), ((), ())), preferred_element_type=jnp.float32
    )


def contract_cols(left_rows, right_rows):
    return lax.dot_general(
        left_rows, right_rows, (((1,), (1,)), ((), ())), preferred_element_type=jnp.float32
    )


def per_source(left_rows, right_rows, dp_count):
    left_split = left_rows.reshape(dp_count, -1, left_rows.shape[1])
    right_split = right_rows.reshape(dp_count, -1, right_rows.shape[1])
    partial_value = jnp.einsum(
        "jra,jrb->jab", left_split, right_split, preferred_element_type=jnp.float32
    )
    rounded = lax.optimization_barrier(partial_value.astype(jnp.bfloat16))
    return jnp.sum(rounded.astype(jnp.float32), axis=0).astype(jnp.bfloat16)


def shards(tokens, grad_out, routes, gates, w_gate, w_up, w_down):
    experts = lax.axis_size("expert")
    dp_count = lax.axis_size("dp")
    tok_count = tokens.shape[0]
    top_count = routes.shape[1]
    slot_cap = min(tok_count, max(2, 3 * tok_count * top_count // (2 * experts)))
    row_total = tok_count * top_count
    flat_routes = routes.reshape(-1)
    flat_gates = gates.reshape(-1)
    onehot = (flat_routes[:, None] == jnp.arange(experts, dtype=jnp.int32)[None, :]).astype(
        jnp.int32
    )
    slot_rank = jnp.sum((jnp.cumsum(onehot, axis=0) - onehot) * onehot, axis=1)
    slot_index = flat_routes * slot_cap + slot_rank
    slot_source = (
        jnp.full((experts * slot_cap,), row_total, jnp.int32)
        .at[slot_index]
        .set(jnp.arange(row_total, dtype=jnp.int32))
    )
    valid = slot_source < row_total
    safe_rows = jnp.where(valid, slot_source, 0)
    token_ids = safe_rows // top_count
    token_slots = jnp.where(valid[:, None], tokens[token_ids], jnp.zeros((), tokens.dtype))
    scaled_slots = jnp.where(
        valid[:, None],
        grad_out[token_ids].astype(jnp.float32) * flat_gates[safe_rows][:, None],
        0.0,
    ).astype(jnp.bfloat16)
    input_cols, scaled_cols = (
        lax.all_to_all(token_slots, "expert", split_axis=0, concat_axis=0, tiled=True),
        lax.all_to_all(scaled_slots, "expert", split_axis=0, concat_axis=0, tiled=True),
    )
    inputs, scaled = (
        lax.all_to_all(input_cols, "dp", split_axis=0, concat_axis=1, tiled=True),
        lax.all_to_all(scaled_cols, "dp", split_axis=0, concat_axis=1, tiled=True),
    )
    full_gate, full_up, full_down = (
        lax.all_gather(w_gate, "dp", axis=1, tiled=True),
        lax.all_gather(w_up, "dp", axis=1, tiled=True),
        lax.all_gather(w_down, "dp", axis=2, tiled=True),
    )
    full_gate = full_gate[0]
    full_up = full_up[0]
    full_down = full_down[0]
    pre_gate = jnp.dot(inputs, full_gate, preferred_element_type=jnp.float32)
    pre_up = jnp.dot(inputs, full_up, preferred_element_type=jnp.float32)
    sigmoid_gate = jax.nn.sigmoid(pre_gate)
    activated = pre_gate * sigmoid_gate
    hidden = (activated * pre_up).astype(jnp.bfloat16)
    back_hidden = contract_cols(scaled, full_down)
    d_up = (back_hidden * activated).astype(jnp.bfloat16)
    d_gate = (back_hidden * pre_up * sigmoid_gate * (1.0 + pre_gate * (1.0 - sigmoid_gate))).astype(
        jnp.bfloat16
    )
    row_grad = (contract_cols(d_gate, full_gate) + contract_cols(d_up, full_up)).astype(
        jnp.bfloat16
    )
    came_back = lax.all_to_all(
        lax.all_to_all(row_grad, "dp", split_axis=1, concat_axis=0, tiled=True),
        "expert",
        split_axis=0,
        concat_axis=0,
        tiled=True,
    )
    picked = came_back[slot_index].astype(jnp.float32)
    d_tokens = jnp.sum(picked.reshape(tok_count, top_count, -1), axis=1).astype(jnp.bfloat16)
    hidden_all = lax.all_gather(hidden, "dp", axis=0, tiled=True)
    grad_down = per_source(hidden_all, scaled_cols, dp_count)
    gate_part = contract_rows(inputs, d_gate).astype(jnp.bfloat16).astype(jnp.float32)
    up_part = contract_rows(inputs, d_up).astype(jnp.bfloat16).astype(jnp.float32)
    gate_sum, up_sum = (
        lax.psum_scatter(
            gate_part.astype(jnp.bfloat16), "dp", scatter_dimension=0, tiled=True
        ).astype(jnp.float32),
        lax.psum_scatter(
            up_part.astype(jnp.bfloat16), "dp", scatter_dimension=0, tiled=True
        ).astype(jnp.float32),
    )
    grad_gate = gate_sum.astype(jnp.bfloat16)
    grad_up = up_sum.astype(jnp.bfloat16)
    return (d_tokens, grad_gate[None], grad_up[None], grad_down[None])


MESH_ID = pl.DeviceIdType.MESH


def contract_first(left, right):
    return lax.dot_general(left, right, (((0,), (0,)), ((), ())), preferred_element_type=jnp.float32)


def fused_kernel(
    tok, cot, routes, gates, wg, wu, wd,
    out_tok, out_gate, out_up, out_down,
    acts, table, w_own, w_far, wd_far, scaled, pre, hidden, d_both,
    row_grad, from_core, from_y, from_z, tok_send, tok_far,
    gate_own, down_own, gate_send, up_send, down_send, gate_far, up_far, down_far,
    x_send, x_recv, z_send, z_recv, y_send, y_recv, c_send, c_recv,
    rc_send, rc_recv, ry_send, ry_recv, rz_send, rz_recv,
):
    e = lax.axis_index("expert")
    d = lax.axis_index("dp")
    core = e % 2
    y_pos = (e // 2) % 2
    z_pos = e // 4
    half = tok.shape[0] // 2
    feats = tok.shape[1]
    width = wg.shape[1]
    x_peer = (e, 1 - d)
    core_peer = (e + 1 - 2 * core, d)
    y_peer = (e + 2 - 4 * y_pos, d)
    z_peers = [((z_pos + k) % 4 * 4 + e % 4, d) for k in (1, 2, 3)]

    def copy(src, dst, send, recv, peer):
        return pltpu.make_async_remote_copy(
            src_ref=src, dst_ref=dst, send_sem=send, recv_sem=recv, device_id=peer, device_id_type=MESH_ID
        )

    barrier = pltpu.get_barrier_semaphore()
    for peer in [x_peer, core_peer, y_peer] + z_peers:
        pl.semaphore_signal(barrier, inc=1, device_id=peer, device_id_type=MESH_ID)

    mine = pl.ds(pl.multiple_of(d * half, half), half)
    theirs = pl.ds(pl.multiple_of((1 - d) * half, half), half)
    acts[0, 0, 0] = tok[mine, :]
    acts[0, 0, 1] = cot[mine, :]
    lanes = lax.broadcasted_iota(jnp.int32, (half, table.shape[-1]), 1)
    chosen, weight = routes[mine, :], gates[mine, :]
    own_table = jnp.zeros((half, table.shape[-1]), jnp.float32)
    for k in range(routes.shape[1]):
        own_table += jnp.where(lanes == chosen[:, k : k + 1], weight[:, k : k + 1], 0.0)
    table[0] = own_table
    pl.semaphore_wait(barrier, 6)

    sends = []

    def start(item):
        item.start()
        sends.append(item)
        return item

    swap_tok = start(copy(tok.at[theirs], acts.at[1, 0, 0], x_send.at[0], x_recv.at[0], x_peer))
    swap_cot = start(copy(cot.at[theirs], acts.at[1, 0, 1], x_send.at[1], x_recv.at[1], x_peer))

    def piece(p, j):
        if p == 2:
            return table.at[j]
        return acts.at[0, j] if p == 0 else acts.at[1, j, p // 3]

    up_peer = ((z_pos + 1) % 4 * 4 + e % 4, d)
    down_peer = ((z_pos + 3) % 4 * 4 + e % 4, d)
    guarded = []

    def line_copy(p, base, src, dst, send, peer):
        return copy(
            piece(p, base + src),
            piece(p, base + dst),
            z_send.at[p, base // 4, send],
            z_recv.at[p, base // 4, dst - 1],
            peer,
        )

    def start_when(condition, item):
        pl.when(condition)(item.start)
        guarded.append((condition, item))

    def line_start(p, base):
        start_when(z_pos < 3, line_copy(p, base, 0, 3, 0, up_peer))
        start_when(z_pos > 0, line_copy(p, base, 0, 1, 1, down_peer))

    def line_step(p, base, j):
        line_copy(p, base, 0, j, 0, up_peer).wait_recv()
        if j == 1:
            start_when((z_pos > 0) & (z_pos < 3), line_copy(p, base, 1, 2, 2, down_peer))
        elif j == 3:
            start_when((z_pos > 0) & (z_pos < 3), line_copy(p, base, 3, 2, 3, up_peer))
        else:
            start_when(z_pos == 1, line_copy(p, base, 2, 3, 4, down_peer))
            start_when(z_pos == 2, line_copy(p, base, 2, 1, 4, up_peer))

    def y_copy(p, j):
        return copy(piece(p, j), piece(p, 4 + j), y_send.at[p, j], y_recv.at[p, j], y_peer)

    def c_copy(p, j):
        return copy(piece(p, j), piece(p, 8 + j), c_send.at[p, j], c_recv.at[p, j], core_peer)

    for p in (2, 0):
        line_start(p, 0)
        start(y_copy(p, 0))
        start(c_copy(p, 0))
    w_own[:, :width] = wg[...]
    w_own[:, width:] = wu[...]
    swap_tok.wait_recv()
    line_start(1, 0)
    start(y_copy(1, 0))
    start(c_copy(1, 0))
    swap_cot.wait_recv()
    start(y_copy(3, 0))
    line_start(3, 0)
    start(c_copy(3, 0))
    w_copies = [
        start(copy(wg, w_far.at[:, pl.ds(0, width)], x_send.at[2], x_recv.at[2], x_peer)),
        start(copy(wu, w_far.at[:, pl.ds(width, width)], x_send.at[3], x_recv.at[3], x_peer)),
    ]
    down_copy = start(copy(wd, wd_far, x_send.at[4], x_recv.at[4], x_peer))

    tile = 4 * half
    blocks = 4

    def rows_of(i):
        return pl.ds(pl.multiple_of(i * tile, tile), tile)

    def scale_rows(h, i):
        rows, group = rows_of(i), pl.ds(i * 4, 4)
        lanes = lax.broadcasted_iota(jnp.int32, (tile, table.shape[-1]), 1)
        column = jnp.sum(
            jnp.where(lanes == e, table[group].reshape(tile, -1), 0.0), axis=1, keepdims=True
        )
        value = acts[h, group, 1].reshape(tile, feats).astype(jnp.float32)
        scaled[h, rows, :] = (value * column).astype(jnp.bfloat16)

    def near_rows(first, count):
        @pl.loop(first, first + count)
        def _(i):
            left = acts[0, pl.ds(i * 4, 4), 0].reshape(tile, feats)
            pre[rows_of(i), :] = jnp.dot(left, w_own[...], preferred_element_type=jnp.float32)
            scale_rows(0, i)

    for j in (1, 3, 2):
        for p in (2, 0):
            line_step(p, 0, j)
            start(y_copy(p, j))
            start(c_copy(p, j))
        if j == 3:
            y_copy(3, 0).wait_recv()
            line_start(3, 4)
            start(c_copy(3, 4))
    for j in (1, 3, 2):
        line_step(1, 0, j)
        start(y_copy(1, j))
        start(c_copy(1, j))
    for j in (0, 1, 3, 2):
        for p in (2, 0):
            y_copy(p, j).wait_recv()
            start(c_copy(p, 4 + j))
    near_rows(0, 2)
    for p in (2, 0):
        for j in range(8):
            c_copy(p, j).wait_recv()
    near_rows(2, 2)
    for j in (1, 3, 2):
        for base in (0, 4):
            line_step(3, base, j)
            start(c_copy(3, base + j))
    for j in (0, 1, 3, 2):
        y_copy(1, j).wait_recv()
        start(c_copy(1, 4 + j))
    for j in range(8):
        c_copy(1, j).wait_recv()
    for item in w_copies:
        item.wait_recv()

    @pl.loop(0, blocks)
    def _(i):
        rows = rows_of(i)
        left = acts[1, pl.ds(i * 4, 4), 0].reshape(tile, feats)
        total = pre[rows, :] + jnp.dot(left, w_far[...], preferred_element_type=jnp.float32)
        pre[rows, :] = total
        gate, up = total[:, :width], total[:, width:]
        hidden[rows, :] = (gate * jax.nn.sigmoid(gate) * up).astype(jnp.bfloat16)

    for j in range(8):
        c_copy(3, j).wait_recv()

    @pl.loop(0, blocks)
    def _(i):
        scale_rows(1, i)

    strip = feats // 4

    def cols_of(i):
        return pl.ds(pl.multiple_of(i * strip, strip), strip)

    @pl.loop(0, 4)
    def _(i):
        down_send[:, cols_of(i)] = contract_first(hidden[...], scaled[1, :, cols_of(i)]).astype(jnp.bfloat16)

    grad_copies = [start(copy(down_send, down_far, x_send.at[5], x_recv.at[5], x_peer))]
    down_copy.wait_recv()

    @pl.loop(0, blocks)
    def _(i):
        rows = rows_of(i)
        back = contract_cols(scaled[0, rows, :], wd[...]) + contract_cols(scaled[1, rows, :], wd_far[...])
        gate, up = pre[rows, :width], pre[rows, width:]
        sig = jax.nn.sigmoid(gate)
        d_both[rows, :width] = (back * up * sig * (1.0 + gate * (1.0 - sig))).astype(jnp.bfloat16)
        d_both[rows, width:] = (back * (gate * sig)).astype(jnp.bfloat16)

    chunk = feats // 2

    def rc_copy(h):
        return copy(row_grad.at[h, pl.ds(8, 8)], from_core.at[h], rc_send.at[h], rc_recv.at[h], core_peer)

    def ry_copy(h):
        return copy(row_grad.at[h, pl.ds(4, 4)], from_y.at[h], ry_send.at[h], ry_recv.at[h], y_peer)

    def rz_copy(h, k):
        return copy(row_grad.at[h, k], from_z.at[h, 3 - k], rz_send.at[h, k - 1], rz_recv.at[h, 3 - k], z_peers[k - 1])

    def rows_back(q, first):
        weights = w_own if q < 2 else w_far
        part = pl.ds(q % 2 * chunk, chunk)

        @pl.loop(first, first + 2)
        def _(i):
            value = contract_cols(d_both[rows_of(i), :], weights[part, :])
            row_grad[q, pl.ds(i * 4, 4)] = value.astype(jnp.bfloat16).reshape(4, half, chunk)

    def to_y(q):
        rows_back(q, 0)
        rc_copy(q).wait_recv()

        @pl.loop(4, 8)
        def _(j):
            near = row_grad[q, j].astype(jnp.float32)
            row_grad[q, j] = (near + from_core[q, j].astype(jnp.float32)).astype(jnp.bfloat16)

        start(ry_copy(q))

    def to_z(q):
        ry_copy(q).wait_recv()

        @pl.loop(0, 4)
        def _(j):
            near = row_grad[q, j].astype(jnp.float32) + from_core[q, j].astype(jnp.float32)
            row_grad[q, j] = (near + from_y[q, j].astype(jnp.float32)).astype(jnp.bfloat16)

        for k in (2, 1, 3):
            start(rz_copy(q, k))

    def finish(q):
        total = row_grad[q, 0].astype(jnp.float32)
        for k in range(3):
            rz_copy(q, 3 - k).wait_recv()
        for k in range(3):
            total = total + from_z[q, k].astype(jnp.float32)
        return total.astype(jnp.bfloat16)

    for q in (2, 3):
        rows_back(q, 2)
        start(rc_copy(q))
    to_y(2)
    for q in (0, 1):
        rows_back(q, 2)
        start(rc_copy(q))
    to_y(3)

    @pl.loop(0, 4)
    def _(i):
        left = acts[1, :, 0, :, cols_of(i)].reshape(16 * half, strip)
        value = contract_first(left, d_both[...]).astype(jnp.bfloat16)
        gate_send[cols_of(i), :] = value[:, :width]
        up_send[cols_of(i), :] = value[:, width:]

    grad_copies.append(start(copy(gate_send, gate_far, x_send.at[6], x_recv.at[6], x_peer)))
    grad_copies.append(start(copy(up_send, up_far, x_send.at[7], x_recv.at[7], x_peer)))

    to_y(0)
    to_z(2)
    to_y(1)
    to_z(3)

    @pl.loop(0, 4)
    def _(i):
        left = acts[0, :, 0, :, cols_of(i)].reshape(16 * half, strip)
        gate_own[cols_of(i), :] = contract_first(left, d_both[...])
        down_own[:, cols_of(i)] = contract_first(hidden[...], scaled[0, :, cols_of(i)])

    to_z(0)
    tok_send[:, :chunk] = finish(2)
    to_z(1)
    tok_send[:, chunk:] = finish(3)
    tok_copy = start(copy(tok_send, tok_far, x_send.at[8], x_recv.at[8], x_peer))
    grad_copies[0].wait_recv()
    out_down[...] = (down_own[...] + down_far[...].astype(jnp.float32)).astype(jnp.bfloat16)
    out_tok[mine, :chunk] = finish(0)
    out_tok[mine, chunk:] = finish(1)
    grad_copies[1].wait_recv()
    out_gate[...] = (gate_own[:, :width] + gate_far[...].astype(jnp.float32)).astype(jnp.bfloat16)
    grad_copies[2].wait_recv()
    out_up[...] = (gate_own[:, width:] + up_far[...].astype(jnp.float32)).astype(jnp.bfloat16)
    tok_copy.wait_recv()
    out_tok[theirs, :] = tok_far[...]
    for item in sends:
        item.wait_send()
    for condition, item in guarded:
        pl.when(condition)(item.wait_send)


def copy_kernel(*refs):
    count = len(refs) // 2
    items = [
        pltpu.make_async_copy(refs[i], refs[count + i], refs[-1].at[i]) for i in range(count)
    ]
    for item in items:
        item.start()
    for item in items:
        item.wait()


def dense_shards(tokens, grad_out, routes, gates, w_gate, w_up, w_down):
    experts = lax.axis_size("expert")
    tok_count, feats = tokens.shape
    width = w_gate.shape[2]
    half = tok_count // 2
    bf, f32 = jnp.bfloat16, jnp.float32
    rows = experts * half
    vmem = pl.BlockSpec(memory_space=pltpu.VMEM)
    dma = pltpu.SemaphoreType.DMA
    results = pl.pallas_call(
        fused_kernel,
        out_shape=(
            jax.ShapeDtypeStruct((tok_count, feats), bf),
            jax.ShapeDtypeStruct((feats, width), bf),
            jax.ShapeDtypeStruct((feats, width), bf),
            jax.ShapeDtypeStruct((width, feats), bf),
        ),
        in_specs=[vmem] * 7,
        out_specs=(vmem,) * 4,
        scratch_shapes=[
            pltpu.VMEM((2, experts, 2, half, feats), bf),
            pltpu.VMEM((experts, half, 128), f32),
            pltpu.VMEM((feats, 2 * width), bf),
            pltpu.VMEM((feats, 2 * width), bf),
            pltpu.VMEM((width, feats), bf),
            pltpu.VMEM((2, rows, feats), bf),
            pltpu.VMEM((rows, 2 * width), f32),
            pltpu.VMEM((rows, width), bf),
            pltpu.VMEM((rows, 2 * width), bf),
            pltpu.VMEM((4, experts, half, feats // 2), bf),
            pltpu.VMEM((4, 8, half, feats // 2), bf),
            pltpu.VMEM((4, 4, half, feats // 2), bf),
            pltpu.VMEM((4, 3, half, feats // 2), bf),
            pltpu.VMEM((half, feats), bf),
            pltpu.VMEM((half, feats), bf),
            pltpu.VMEM((feats, 2 * width), f32),
            pltpu.VMEM((width, feats), f32),
            pltpu.VMEM((feats, width), bf),
            pltpu.VMEM((feats, width), bf),
            pltpu.VMEM((width, feats), bf),
            pltpu.VMEM((feats, width), bf),
            pltpu.VMEM((feats, width), bf),
            pltpu.VMEM((width, feats), bf),
            dma((9,)), dma((9,)),
            dma((4, 2, 5)), dma((4, 2, 3)),
            dma((4, 4)), dma((4, 4)),
            dma((4, 8)), dma((4, 8)),
            dma((4,)), dma((4,)),
            dma((4,)), dma((4,)),
            dma((4, 3)), dma((4, 3)),
        ],
        compiler_params=pltpu.CompilerParams(
            collective_id=0, has_side_effects=True, vmem_limit_bytes=60 * 1024 * 1024
        ),
        cost_estimate=pl.CostEstimate(
            flops=16 * rows * 2 * feats * width, bytes_accessed=8 * 1024 * 1024, transcendentals=rows * width
        ),
    )(tokens, grad_out, routes, gates, w_gate[0], w_up[0], w_down[0])
    anywhere = pl.BlockSpec(memory_space=pl.ANY)
    d_tokens, grad_gate, grad_up, grad_down = pl.pallas_call(
        copy_kernel,
        out_shape=tuple(jax.ShapeDtypeStruct(r.shape, r.dtype) for r in results),
        in_specs=[anywhere] * 4,
        out_specs=(anywhere,) * 4,
        scratch_shapes=[dma((4,))],
    )(*results)
    return (d_tokens, grad_gate[None], grad_up[None], grad_down[None])


def solution(mesh):
    small = mesh.shape["expert"] == 16 and mesh.shape["dp"] == 2
    return jax.shard_map(
        dense_shards if small else shards,
        mesh=mesh,
        in_specs=(
            P("expert", "dp"),
            P("expert", "dp"),
            P("expert", None),
            P("expert", None),
            P("expert", "dp", None),
            P("expert", "dp", None),
            P("expert", None, "dp"),
        ),
        out_specs=(
            P("expert", "dp"),
            P("expert", "dp", None),
            P("expert", "dp", None),
            P("expert", None, "dp"),
        ),
        check_vma=False,
    )
```

```python
import jax
import jax.numpy as jnp
from jax import lax
from jax.experimental import pallas as pl
from jax.experimental.pallas import tpu as pltpu
from jax.sharding import PartitionSpec as P


def contract_rows(left_rows, right_rows):
    return lax.dot_general(
        left_rows, right_rows, (((0,), (0,)), ((), ())), preferred_element_type=jnp.float32
    )


def contract_cols(left_rows, right_rows):
    return lax.dot_general(
        left_rows, right_rows, (((1,), (1,)), ((), ())), preferred_element_type=jnp.float32
    )


def per_source(left_rows, right_rows, dp_count):
    left_split = left_rows.reshape(dp_count, -1, left_rows.shape[1])
    right_split = right_rows.reshape(dp_count, -1, right_rows.shape[1])
    partial_value = jnp.einsum(
        "jra,jrb->jab", left_split, right_split, preferred_element_type=jnp.float32
    )
    rounded = lax.optimization_barrier(partial_value.astype(jnp.bfloat16))
    return jnp.sum(rounded.astype(jnp.float32), axis=0).astype(jnp.bfloat16)


def shards(tokens, grad_out, routes, gates, w_gate, w_up, w_down):
    experts = lax.axis_size("expert")
    dp_count = lax.axis_size("dp")
    tok_count = tokens.shape[0]
    top_count = routes.shape[1]
    slot_cap = min(tok_count, max(2, 3 * tok_count * top_count // (2 * experts)))
    row_total = tok_count * top_count
    flat_routes = routes.reshape(-1)
    flat_gates = gates.reshape(-1)
    onehot = (flat_routes[:, None] == jnp.arange(experts, dtype=jnp.int32)[None, :]).astype(
        jnp.int32
    )
    slot_rank = jnp.sum((jnp.cumsum(onehot, axis=0) - onehot) * onehot, axis=1)
    slot_index = flat_routes * slot_cap + slot_rank
    slot_source = (
        jnp.full((experts * slot_cap,), row_total, jnp.int32)
        .at[slot_index]
        .set(jnp.arange(row_total, dtype=jnp.int32))
    )
    valid = slot_source < row_total
    safe_rows = jnp.where(valid, slot_source, 0)
    token_ids = safe_rows // top_count
    token_slots = jnp.where(valid[:, None], tokens[token_ids], jnp.zeros((), tokens.dtype))
    scaled_slots = jnp.where(
        valid[:, None],
        grad_out[token_ids].astype(jnp.float32) * flat_gates[safe_rows][:, None],
        0.0,
    ).astype(jnp.bfloat16)
    input_cols, scaled_cols = (
        lax.all_to_all(token_slots, "expert", split_axis=0, concat_axis=0, tiled=True),
        lax.all_to_all(scaled_slots, "expert", split_axis=0, concat_axis=0, tiled=True),
    )
    inputs, scaled = (
        lax.all_to_all(input_cols, "dp", split_axis=0, concat_axis=1, tiled=True),
        lax.all_to_all(scaled_cols, "dp", split_axis=0, concat_axis=1, tiled=True),
    )
    full_gate, full_up, full_down = (
        lax.all_gather(w_gate, "dp", axis=1, tiled=True),
        lax.all_gather(w_up, "dp", axis=1, tiled=True),
        lax.all_gather(w_down, "dp", axis=2, tiled=True),
    )
    full_gate = full_gate[0]
    full_up = full_up[0]
    full_down = full_down[0]
    pre_gate = jnp.dot(inputs, full_gate, preferred_element_type=jnp.float32)
    pre_up = jnp.dot(inputs, full_up, preferred_element_type=jnp.float32)
    sigmoid_gate = jax.nn.sigmoid(pre_gate)
    activated = pre_gate * sigmoid_gate
    hidden = (activated * pre_up).astype(jnp.bfloat16)
    back_hidden = contract_cols(scaled, full_down)
    d_up = (back_hidden * activated).astype(jnp.bfloat16)
    d_gate = (back_hidden * pre_up * sigmoid_gate * (1.0 + pre_gate * (1.0 - sigmoid_gate))).astype(
        jnp.bfloat16
    )
    row_grad = (contract_cols(d_gate, full_gate) + contract_cols(d_up, full_up)).astype(
        jnp.bfloat16
    )
    came_back = lax.all_to_all(
        lax.all_to_all(row_grad, "dp", split_axis=1, concat_axis=0, tiled=True),
        "expert",
        split_axis=0,
        concat_axis=0,
        tiled=True,
    )
    picked = came_back[slot_index].astype(jnp.float32)
    d_tokens = jnp.sum(picked.reshape(tok_count, top_count, -1), axis=1).astype(jnp.bfloat16)
    hidden_all = lax.all_gather(hidden, "dp", axis=0, tiled=True)
    grad_down = per_source(hidden_all, scaled_cols, dp_count)
    gate_part = contract_rows(inputs, d_gate).astype(jnp.bfloat16).astype(jnp.float32)
    up_part = contract_rows(inputs, d_up).astype(jnp.bfloat16).astype(jnp.float32)
    gate_sum, up_sum = (
        lax.psum_scatter(
            gate_part.astype(jnp.bfloat16), "dp", scatter_dimension=0, tiled=True
        ).astype(jnp.float32),
        lax.psum_scatter(
            up_part.astype(jnp.bfloat16), "dp", scatter_dimension=0, tiled=True
        ).astype(jnp.float32),
    )
    grad_gate = gate_sum.astype(jnp.bfloat16)
    grad_up = up_sum.astype(jnp.bfloat16)
    return (d_tokens, grad_gate[None], grad_up[None], grad_down[None])


MESH_ID = pl.DeviceIdType.MESH


def contract_first(left, right):
    return lax.dot_general(left, right, (((0,), (0,)), ((), ())), preferred_element_type=jnp.float32)


def fused_kernel(
    tok, cot, routes, gates, wg, wu, wd,
    out_tok, out_gate, out_up, out_down,
    acts, table, w_own, w_far, wd_far, scaled, pre, hidden, d_both,
    row_grad, from_core, from_y, from_z, tok_send, tok_far,
    both_own, down_own, both_send, down_send, both_far, down_far, named_rows, gate_rows,
    x_send, x_recv, z_send, z_recv, y_send, y_recv, c_send, c_recv,
    rc_send, rc_recv, ry_send, ry_recv, rz_send, rz_recv,
):
    e = lax.axis_index("expert")
    d = lax.axis_index("dp")
    core = e % 2
    y_pos = (e // 2) % 2
    z_pos = e // 4
    half = tok.shape[0] // 2
    feats = tok.shape[1]
    width = wg.shape[1]
    x_peer = (e, 1 - d)
    core_peer = (e + 1 - 2 * core, d)
    y_peer = (e + 2 - 4 * y_pos, d)
    z_peers = [((z_pos + k) % 4 * 4 + e % 4, d) for k in (1, 2, 3)]

    def copy(src, dst, send, recv, peer):
        return pltpu.make_async_remote_copy(
            src_ref=src, dst_ref=dst, send_sem=send, recv_sem=recv, device_id=peer, device_id_type=MESH_ID
        )

    barrier = pltpu.get_barrier_semaphore()
    for peer in [x_peer, core_peer, y_peer] + z_peers:
        pl.semaphore_signal(barrier, inc=1, device_id=peer, device_id_type=MESH_ID)

    mine = pl.ds(pl.multiple_of(d * half, half), half)
    theirs = pl.ds(pl.multiple_of((1 - d) * half, half), half)
    acts[0, 0, 0] = tok[mine, :]
    acts[0, 0, 1] = cot[mine, :]
    lanes = lax.broadcasted_iota(jnp.int32, (half, table.shape[-1]), 1)
    named_rows[...] = jnp.transpose(routes[...])
    gate_rows[...] = jnp.transpose(gates[...])
    chosen, weight = named_rows[mine, :], gate_rows[mine, :]
    own_table = jnp.zeros((half, table.shape[-1]), jnp.float32)
    for k in range(routes.shape[0]):
        own_table += jnp.where(lanes == chosen[:, k : k + 1], weight[:, k : k + 1], 0.0)
    table[0] = own_table
    pl.semaphore_wait(barrier, 6)

    sends = []

    def start(item):
        item.start()
        sends.append(item)
        return item

    swap_tok = start(copy(tok.at[theirs], acts.at[1, 0, 0], x_send.at[0], x_recv.at[0], x_peer))
    swap_cot = start(copy(cot.at[theirs], acts.at[1, 0, 1], x_send.at[1], x_recv.at[1], x_peer))

    def piece(p, j):
        if p == 2:
            return table.at[j]
        return acts.at[0, j] if p == 0 else acts.at[1, j, p // 3]

    up_peer = ((z_pos + 1) % 4 * 4 + e % 4, d)
    down_peer = ((z_pos + 3) % 4 * 4 + e % 4, d)
    guarded = []

    def line_copy(p, base, src, dst, send, peer):
        return copy(
            piece(p, base + src),
            piece(p, base + dst),
            z_send.at[p, base // 4, send],
            z_recv.at[p, base // 4, dst - 1],
            peer,
        )

    def start_when(condition, item):
        pl.when(condition)(item.start)
        guarded.append((condition, item))

    def line_start(p, base):
        start_when(z_pos < 3, line_copy(p, base, 0, 3, 0, up_peer))
        start_when(z_pos > 0, line_copy(p, base, 0, 1, 1, down_peer))

    def line_step(p, base, j):
        line_copy(p, base, 0, j, 0, up_peer).wait_recv()
        if j == 1:
            start_when((z_pos > 0) & (z_pos < 3), line_copy(p, base, 1, 2, 2, down_peer))
        elif j == 3:
            start_when((z_pos > 0) & (z_pos < 3), line_copy(p, base, 3, 2, 3, up_peer))
        else:
            start_when(z_pos == 1, line_copy(p, base, 2, 3, 4, down_peer))
            start_when(z_pos == 2, line_copy(p, base, 2, 1, 4, up_peer))

    def y_copy(p, j):
        return copy(piece(p, j), piece(p, 4 + j), y_send.at[p, j], y_recv.at[p, j], y_peer)

    def c_copy(p, j):
        return copy(piece(p, j), piece(p, 8 + j), c_send.at[p, j], c_recv.at[p, j], core_peer)

    for p in (2, 0):
        line_start(p, 0)
        start(y_copy(p, 0))
        start(c_copy(p, 0))
    w_own[:, :width] = wg[...]
    w_own[:, width:] = wu[...]
    w_copies = [start(copy(wg, w_far.at[:, pl.ds(0, width)], x_send.at[2], x_recv.at[2], x_peer))]
    swap_tok.wait_recv()
    line_start(1, 0)
    start(y_copy(1, 0))
    start(c_copy(1, 0))
    swap_cot.wait_recv()
    start(y_copy(3, 0))
    line_start(3, 0)
    start(c_copy(3, 0))
    w_copies.append(
        start(copy(wu, w_far.at[:, pl.ds(width, width)], x_send.at[3], x_recv.at[3], x_peer))
    )
    down_copy = start(copy(wd, wd_far, x_send.at[4], x_recv.at[4], x_peer))

    tile = 4 * half
    blocks = 4

    def rows_of(i):
        return pl.ds(pl.multiple_of(i * tile, tile), tile)

    def scale_rows(h, i):
        rows, group = rows_of(i), pl.ds(i * 4, 4)
        lanes = lax.broadcasted_iota(jnp.int32, (tile, table.shape[-1]), 1)
        column = jnp.sum(
            jnp.where(lanes == e, table[group].reshape(tile, -1), 0.0), axis=1, keepdims=True
        )
        value = acts[h, group, 1].reshape(tile, feats).astype(jnp.float32)
        scaled[h, rows, :] = (value * column).astype(jnp.bfloat16)

    def near_rows(first, count):
        @pl.loop(first, first + count)
        def _(i):
            left = acts[0, pl.ds(i * 4, 4), 0].reshape(tile, feats)
            pre[rows_of(i), :] = jnp.dot(left, w_own[...], preferred_element_type=jnp.float32)
            scale_rows(0, i)

    for j in (1, 3, 2):
        for p in (2, 0):
            line_step(p, 0, j)
            start(y_copy(p, j))
            start(c_copy(p, j))
        if j == 3:
            y_copy(3, 0).wait_recv()
            line_start(3, 4)
            start(c_copy(3, 4))
    for j in (1, 3, 2):
        line_step(1, 0, j)
        start(y_copy(1, j))
        start(c_copy(1, j))
    for j in (0, 1, 3, 2):
        for p in (2, 0):
            y_copy(p, j).wait_recv()
            start(c_copy(p, 4 + j))
    near_rows(0, 2)
    for p in (2, 0):
        for j in range(8):
            c_copy(p, j).wait_recv()
    near_rows(2, 2)
    for j in (1, 3, 2):
        for base in (0, 4):
            line_step(3, base, j)
            start(c_copy(3, base + j))
    for j in (0, 1, 3, 2):
        y_copy(1, j).wait_recv()
        start(c_copy(1, 4 + j))
    for j in range(8):
        c_copy(1, j).wait_recv()
    for item in w_copies:
        item.wait_recv()

    @pl.loop(0, blocks)
    def _(i):
        rows = rows_of(i)
        left = acts[1, pl.ds(i * 4, 4), 0].reshape(tile, feats)
        total = pre[rows, :] + jnp.dot(left, w_far[...], preferred_element_type=jnp.float32)
        pre[rows, :] = total
        gate, up = total[:, :width], total[:, width:]
        hidden[rows, :] = (gate * jax.nn.sigmoid(gate) * up).astype(jnp.bfloat16)

    for j in range(8):
        c_copy(3, j).wait_recv()

    @pl.loop(0, blocks)
    def _(i):
        scale_rows(1, i)

    strip = feats // 4

    def cols_of(i):
        return pl.ds(pl.multiple_of(i * strip, strip), strip)

    @pl.loop(0, 4)
    def _(i):
        down_send[:, cols_of(i)] = contract_first(hidden[...], scaled[1, :, cols_of(i)]).astype(jnp.bfloat16)

    grad_copies = [start(copy(down_send, down_far, x_send.at[5], x_recv.at[5], x_peer))]
    down_copy.wait_recv()

    @pl.loop(0, blocks)
    def _(i):
        rows = rows_of(i)
        back = contract_cols(scaled[0, rows, :], wd[...]) + contract_cols(scaled[1, rows, :], wd_far[...])
        gate, up = pre[rows, :width], pre[rows, width:]
        sig = jax.nn.sigmoid(gate)
        d_both[rows, :width] = (back * up * sig * (1.0 + gate * (1.0 - sig))).astype(jnp.bfloat16)
        d_both[rows, width:] = (back * (gate * sig)).astype(jnp.bfloat16)

    chunk = feats // 2

    def rc_copy(h):
        return copy(row_grad.at[h, pl.ds(8, 8)], from_core.at[h], rc_send.at[h], rc_recv.at[h], core_peer)

    def ry_copy(h):
        return copy(row_grad.at[h, pl.ds(4, 4)], from_y.at[h], ry_send.at[h], ry_recv.at[h], y_peer)

    def rz_copy(h, k):
        return copy(row_grad.at[h, k], from_z.at[h, 3 - k], rz_send.at[h, k - 1], rz_recv.at[h, 3 - k], z_peers[k - 1])

    def rows_back(q, first):
        weights = w_own if q < 2 else w_far
        part = pl.ds(q % 2 * chunk, chunk)

        @pl.loop(first, first + 2)
        def _(i):
            value = contract_cols(d_both[rows_of(i), :], weights[part, :])
            row_grad[q, pl.ds(i * 4, 4)] = value.astype(jnp.bfloat16).reshape(4, half, chunk)

    def to_y(q):
        rows_back(q, 0)
        rc_copy(q).wait_recv()

        @pl.loop(4, 8)
        def _(j):
            near = row_grad[q, j].astype(jnp.float32)
            row_grad[q, j] = (near + from_core[q, j].astype(jnp.float32)).astype(jnp.bfloat16)

        start(ry_copy(q))

    def to_z(q):
        ry_copy(q).wait_recv()

        @pl.loop(0, 4)
        def _(j):
            near = row_grad[q, j].astype(jnp.float32) + from_core[q, j].astype(jnp.float32)
            row_grad[q, j] = (near + from_y[q, j].astype(jnp.float32)).astype(jnp.bfloat16)

        for k in (2, 1, 3):
            start(rz_copy(q, k))

    def finish(q):
        total = row_grad[q, 0].astype(jnp.float32)
        for k in range(3):
            rz_copy(q, 3 - k).wait_recv()
        for k in range(3):
            total = total + from_z[q, k].astype(jnp.float32)
        return total.astype(jnp.bfloat16)

    def far_grads(part):
        @pl.loop(2 * part, 2 * part + 2)
        def _(i):
            left = acts[1, :, 0, :, cols_of(i)].reshape(16 * half, strip)
            both_send[cols_of(i), :] = contract_first(left, d_both[...]).astype(jnp.bfloat16)

        rows = pl.ds(part * chunk, chunk)
        grad_copies.append(
            start(copy(both_send.at[rows], both_far.at[rows], x_send.at[6 + part], x_recv.at[6 + part], x_peer))
        )

    for q in (2, 3):
        rows_back(q, 2)
        start(rc_copy(q))
    to_y(2)
    far_grads(0)
    for q in (0, 1):
        rows_back(q, 2)
        start(rc_copy(q))
    to_y(3)
    far_grads(1)
    to_y(0)
    to_z(2)
    to_y(1)
    to_z(3)

    @pl.loop(0, 4)
    def _(i):
        left = acts[0, :, 0, :, cols_of(i)].reshape(16 * half, strip)
        both_own[cols_of(i), :] = contract_first(left, d_both[...])
        down_own[:, cols_of(i)] = contract_first(hidden[...], scaled[0, :, cols_of(i)])

    to_z(0)
    tok_send[:, :chunk] = finish(2)
    to_z(1)
    tok_send[:, chunk:] = finish(3)
    tok_copy = start(copy(tok_send, tok_far, x_send.at[8], x_recv.at[8], x_peer))
    grad_copies[0].wait_recv()
    out_down[...] = (down_own[...] + down_far[...].astype(jnp.float32)).astype(jnp.bfloat16)
    out_tok[mine, :chunk] = finish(0)
    out_tok[mine, chunk:] = finish(1)
    for part in range(2):
        rows = pl.ds(part * chunk, chunk)
        grad_copies[1 + part].wait_recv()
        total = (both_own[rows, :] + both_far[rows, :].astype(jnp.float32)).astype(jnp.bfloat16)
        out_gate[rows, :] = total[:, :width]
        out_up[rows, :] = total[:, width:]
    tok_copy.wait_recv()
    out_tok[theirs, :] = tok_far[...]
    for item in sends:
        item.wait_send()
    for condition, item in guarded:
        pl.when(condition)(item.wait_send)


def copy_kernel(*refs):
    count = len(refs) // 2
    for i in range(count):
        refs[count + i][...] = refs[i][...]


def dense_shards(tokens, grad_out, routes, gates, w_gate, w_up, w_down):
    experts = lax.axis_size("expert")
    tok_count, feats = tokens.shape
    width = w_gate.shape[2]
    half = tok_count // 2
    bf, f32 = jnp.bfloat16, jnp.float32
    rows = experts * half
    vmem = pl.BlockSpec(memory_space=pltpu.VMEM)
    dma = pltpu.SemaphoreType.DMA
    results = pl.pallas_call(
        fused_kernel,
        out_shape=(
            jax.ShapeDtypeStruct((tok_count, feats), bf),
            jax.ShapeDtypeStruct((feats, width), bf),
            jax.ShapeDtypeStruct((feats, width), bf),
            jax.ShapeDtypeStruct((width, feats), bf),
        ),
        in_specs=[vmem] * 7,
        out_specs=(vmem,) * 4,
        scratch_shapes=[
            pltpu.VMEM((2, experts, 2, half, feats), bf),
            pltpu.VMEM((experts, half, 128), f32),
            pltpu.VMEM((feats, 2 * width), bf),
            pltpu.VMEM((feats, 2 * width), bf),
            pltpu.VMEM((width, feats), bf),
            pltpu.VMEM((2, rows, feats), bf),
            pltpu.VMEM((rows, 2 * width), f32),
            pltpu.VMEM((rows, width), bf),
            pltpu.VMEM((rows, 2 * width), bf),
            pltpu.VMEM((4, experts, half, feats // 2), bf),
            pltpu.VMEM((4, 8, half, feats // 2), bf),
            pltpu.VMEM((4, 4, half, feats // 2), bf),
            pltpu.VMEM((4, 3, half, feats // 2), bf),
            pltpu.VMEM((half, feats), bf),
            pltpu.VMEM((half, feats), bf),
            pltpu.VMEM((feats, 2 * width), f32),
            pltpu.VMEM((width, feats), f32),
            pltpu.VMEM((feats, 2 * width), bf),
            pltpu.VMEM((width, feats), bf),
            pltpu.VMEM((feats, 2 * width), bf),
            pltpu.VMEM((width, feats), bf),
            pltpu.VMEM(routes.shape, jnp.int32),
            pltpu.VMEM(gates.shape, f32),
            dma((9,)), dma((9,)),
            dma((4, 2, 5)), dma((4, 2, 3)),
            dma((4, 4)), dma((4, 4)),
            dma((4, 8)), dma((4, 8)),
            dma((4,)), dma((4,)),
            dma((4,)), dma((4,)),
            dma((4, 3)), dma((4, 3)),
        ],
        compiler_params=pltpu.CompilerParams(
            collective_id=0, has_side_effects=True, vmem_limit_bytes=60 * 1024 * 1024
        ),
        cost_estimate=pl.CostEstimate(
            flops=16 * rows * 2 * feats * width, bytes_accessed=8 * 1024 * 1024, transcendentals=rows * width
        ),
    )(tokens, grad_out, routes.T, gates.T, w_gate[0], w_up[0], w_down[0])
    steps = 4
    specs = [pl.BlockSpec((r.shape[0] // steps, r.shape[1]), lambda i: (i, 0)) for r in results]
    d_tokens, grad_gate, grad_up, grad_down = pl.pallas_call(
        copy_kernel,
        grid=(steps,),
        out_shape=tuple(jax.ShapeDtypeStruct(r.shape, r.dtype) for r in results),
        in_specs=specs,
        out_specs=tuple(specs),
        compiler_params=pltpu.CompilerParams(vmem_limit_bytes=60 * 1024 * 1024),
    )(*results)
    return (d_tokens, grad_gate[None], grad_up[None], grad_down[None])


def solution(mesh):
    small = mesh.shape["expert"] == 16 and mesh.shape["dp"] == 2
    return jax.shard_map(
        dense_shards if small else shards,
        mesh=mesh,
        in_specs=(
            P("expert", "dp"),
            P("expert", "dp"),
            P("expert", None),
            P("expert", None),
            P("expert", "dp", None),
            P("expert", "dp", None),
            P("expert", None, "dp"),
        ),
        out_specs=(
            P("expert", "dp"),
            P("expert", "dp", None),
            P("expert", "dp", None),
            P("expert", None, "dp"),
        ),
        check_vma=False,
    )
```

```python
import jax
import jax.numpy as jnp
from jax import lax
from jax.experimental import pallas as pl
from jax.experimental.pallas import tpu as pltpu
from jax.sharding import PartitionSpec as P


def contract_rows(left_rows, right_rows):
    return lax.dot_general(
        left_rows, right_rows, (((0,), (0,)), ((), ())), preferred_element_type=jnp.float32
    )


def contract_cols(left_rows, right_rows):
    return lax.dot_general(
        left_rows, right_rows, (((1,), (1,)), ((), ())), preferred_element_type=jnp.float32
    )


def per_source(left_rows, right_rows, dp_count):
    left_split = left_rows.reshape(dp_count, -1, left_rows.shape[1])
    right_split = right_rows.reshape(dp_count, -1, right_rows.shape[1])
    partial_value = jnp.einsum(
        "jra,jrb->jab", left_split, right_split, preferred_element_type=jnp.float32
    )
    rounded = lax.optimization_barrier(partial_value.astype(jnp.bfloat16))
    return jnp.sum(rounded.astype(jnp.float32), axis=0).astype(jnp.bfloat16)


def shards(tokens, grad_out, routes, gates, w_gate, w_up, w_down):
    experts = lax.axis_size("expert")
    dp_count = lax.axis_size("dp")
    tok_count = tokens.shape[0]
    top_count = routes.shape[1]
    slot_cap = min(tok_count, max(2, 3 * tok_count * top_count // (2 * experts)))
    row_total = tok_count * top_count
    flat_routes = routes.reshape(-1)
    flat_gates = gates.reshape(-1)
    onehot = (flat_routes[:, None] == jnp.arange(experts, dtype=jnp.int32)[None, :]).astype(
        jnp.int32
    )
    slot_rank = jnp.sum((jnp.cumsum(onehot, axis=0) - onehot) * onehot, axis=1)
    slot_index = flat_routes * slot_cap + slot_rank
    slot_source = (
        jnp.full((experts * slot_cap,), row_total, jnp.int32)
        .at[slot_index]
        .set(jnp.arange(row_total, dtype=jnp.int32))
    )
    valid = slot_source < row_total
    safe_rows = jnp.where(valid, slot_source, 0)
    token_ids = safe_rows // top_count
    token_slots = jnp.where(valid[:, None], tokens[token_ids], jnp.zeros((), tokens.dtype))
    scaled_slots = jnp.where(
        valid[:, None],
        grad_out[token_ids].astype(jnp.float32) * flat_gates[safe_rows][:, None],
        0.0,
    ).astype(jnp.bfloat16)
    input_cols, scaled_cols = (
        lax.all_to_all(token_slots, "expert", split_axis=0, concat_axis=0, tiled=True),
        lax.all_to_all(scaled_slots, "expert", split_axis=0, concat_axis=0, tiled=True),
    )
    inputs, scaled = (
        lax.all_to_all(input_cols, "dp", split_axis=0, concat_axis=1, tiled=True),
        lax.all_to_all(scaled_cols, "dp", split_axis=0, concat_axis=1, tiled=True),
    )
    full_gate, full_up, full_down = (
        lax.all_gather(w_gate, "dp", axis=1, tiled=True),
        lax.all_gather(w_up, "dp", axis=1, tiled=True),
        lax.all_gather(w_down, "dp", axis=2, tiled=True),
    )
    full_gate = full_gate[0]
    full_up = full_up[0]
    full_down = full_down[0]
    pre_gate = jnp.dot(inputs, full_gate, preferred_element_type=jnp.float32)
    pre_up = jnp.dot(inputs, full_up, preferred_element_type=jnp.float32)
    sigmoid_gate = jax.nn.sigmoid(pre_gate)
    activated = pre_gate * sigmoid_gate
    hidden = (activated * pre_up).astype(jnp.bfloat16)
    back_hidden = contract_cols(scaled, full_down)
    d_up = (back_hidden * activated).astype(jnp.bfloat16)
    d_gate = (back_hidden * pre_up * sigmoid_gate * (1.0 + pre_gate * (1.0 - sigmoid_gate))).astype(
        jnp.bfloat16
    )
    row_grad = (contract_cols(d_gate, full_gate) + contract_cols(d_up, full_up)).astype(
        jnp.bfloat16
    )
    came_back = lax.all_to_all(
        lax.all_to_all(row_grad, "dp", split_axis=1, concat_axis=0, tiled=True),
        "expert",
        split_axis=0,
        concat_axis=0,
        tiled=True,
    )
    picked = came_back[slot_index].astype(jnp.float32)
    d_tokens = jnp.sum(picked.reshape(tok_count, top_count, -1), axis=1).astype(jnp.bfloat16)
    hidden_all = lax.all_gather(hidden, "dp", axis=0, tiled=True)
    grad_down = per_source(hidden_all, scaled_cols, dp_count)
    gate_part = contract_rows(inputs, d_gate).astype(jnp.bfloat16).astype(jnp.float32)
    up_part = contract_rows(inputs, d_up).astype(jnp.bfloat16).astype(jnp.float32)
    gate_sum, up_sum = (
        lax.psum_scatter(
            gate_part.astype(jnp.bfloat16), "dp", scatter_dimension=0, tiled=True
        ).astype(jnp.float32),
        lax.psum_scatter(
            up_part.astype(jnp.bfloat16), "dp", scatter_dimension=0, tiled=True
        ).astype(jnp.float32),
    )
    grad_gate = gate_sum.astype(jnp.bfloat16)
    grad_up = up_sum.astype(jnp.bfloat16)
    return (d_tokens, grad_gate[None], grad_up[None], grad_down[None])


MESH_ID = pl.DeviceIdType.MESH


def contract_first(left, right):
    return lax.dot_general(left, right, (((0,), (0,)), ((), ())), preferred_element_type=jnp.float32)


def fused_kernel(
    tok, cot, routes, gates, wg, wu, wd,
    out_tok, out_gate, out_up, out_down,
    acts, table, w_own, w_far, wd_far, scaled, pre, hidden, d_both,
    row_grad, from_core, from_y, from_z, tok_send, tok_far,
    both_own, down_own, both_send, down_send, both_far, down_far, named_rows, gate_rows,
    back_near, wd_own, local_sem,
    x_send, x_recv, z_send, z_recv, y_send, y_recv, c_send, c_recv,
    rc_send, rc_recv, ry_send, ry_recv, rz_send, rz_recv,
):
    e = lax.axis_index("expert")
    d = lax.axis_index("dp")
    core = e % 2
    y_pos = (e // 2) % 2
    z_pos = e // 4
    half = tok.shape[0] // 2
    feats = tok.shape[1]
    width = wg.shape[1]
    x_peer = (e, 1 - d)
    core_peer = (e + 1 - 2 * core, d)
    y_peer = (e + 2 - 4 * y_pos, d)
    z_peers = [((z_pos + k) % 4 * 4 + e % 4, d) for k in (1, 2, 3)]

    def copy(src, dst, send, recv, peer):
        return pltpu.make_async_remote_copy(
            src_ref=src, dst_ref=dst, send_sem=send, recv_sem=recv, device_id=peer, device_id_type=MESH_ID
        )

    barrier = pltpu.get_barrier_semaphore()
    for peer in [x_peer, core_peer, y_peer] + z_peers:
        pl.semaphore_signal(barrier, inc=1, device_id=peer, device_id_type=MESH_ID)

    mine = pl.ds(pl.multiple_of(d * half, half), half)
    theirs = pl.ds(pl.multiple_of((1 - d) * half, half), half)
    own_copies = [
        pltpu.make_async_copy(src, dst, local_sem.at[i])
        for i, (src, dst) in enumerate(
            [
                (tok.at[mine], acts.at[0, 0, 0]),
                (cot.at[mine], acts.at[0, 0, 1]),
                (wg, w_own.at[:, pl.ds(0, width)]),
                (wu, w_own.at[:, pl.ds(width, width)]),
                (wd, wd_own),
            ]
        )
    ]
    for item in own_copies:
        item.start()
    lanes = lax.broadcasted_iota(jnp.int32, (half, table.shape[-1]), 1)
    named_rows[...] = jnp.transpose(routes[...])
    gate_rows[...] = jnp.transpose(gates[...])
    chosen, weight = named_rows[mine, :], gate_rows[mine, :]
    own_table = jnp.zeros((half, table.shape[-1]), jnp.float32)
    for k in range(routes.shape[0]):
        own_table += jnp.where(lanes == chosen[:, k : k + 1], weight[:, k : k + 1], 0.0)
    table[0] = own_table
    pl.semaphore_wait(barrier, 6)

    sends = []

    def start(item):
        item.start()
        sends.append(item)
        return item

    swap_tok = start(copy(tok.at[theirs], acts.at[1, 0, 0], x_send.at[0], x_recv.at[0], x_peer))
    swap_cot = start(copy(cot.at[theirs], acts.at[1, 0, 1], x_send.at[1], x_recv.at[1], x_peer))

    def piece(p, j):
        if p == 2:
            return table.at[j]
        return acts.at[0, j] if p == 0 else acts.at[1, j, p // 3]

    up_peer = ((z_pos + 1) % 4 * 4 + e % 4, d)
    down_peer = ((z_pos + 3) % 4 * 4 + e % 4, d)
    guarded = []

    def line_copy(p, base, src, dst, send, peer):
        return copy(
            piece(p, base + src),
            piece(p, base + dst),
            z_send.at[p, base // 4, send],
            z_recv.at[p, base // 4, dst - 1],
            peer,
        )

    def start_when(condition, item):
        pl.when(condition)(item.start)
        guarded.append((condition, item))

    def line_start(p, base):
        start_when(z_pos < 3, line_copy(p, base, 0, 3, 0, up_peer))
        start_when(z_pos > 0, line_copy(p, base, 0, 1, 1, down_peer))

    def line_step(p, base, j):
        line_copy(p, base, 0, j, 0, up_peer).wait_recv()
        if j == 1:
            start_when((z_pos > 0) & (z_pos < 3), line_copy(p, base, 1, 2, 2, down_peer))
        elif j == 3:
            start_when((z_pos > 0) & (z_pos < 3), line_copy(p, base, 3, 2, 3, up_peer))
        else:
            start_when(z_pos == 1, line_copy(p, base, 2, 3, 4, down_peer))
            start_when(z_pos == 2, line_copy(p, base, 2, 1, 4, up_peer))

    def y_copy(p, j):
        return copy(piece(p, j), piece(p, 4 + j), y_send.at[p, j], y_recv.at[p, j], y_peer)

    def c_copy(p, j):
        return copy(piece(p, j), piece(p, 8 + j), c_send.at[p, j], c_recv.at[p, j], core_peer)

    own_copies[0].wait()
    own_copies[1].wait()
    for p in (2, 0):
        line_start(p, 0)
        start(y_copy(p, 0))
        start(c_copy(p, 0))
    w_copies = [start(copy(wg, w_far.at[:, pl.ds(0, width)], x_send.at[2], x_recv.at[2], x_peer))]
    swap_tok.wait_recv()
    line_start(1, 0)
    start(y_copy(1, 0))
    start(c_copy(1, 0))
    swap_cot.wait_recv()
    start(y_copy(3, 0))
    line_start(3, 0)
    start(c_copy(3, 0))
    w_copies.append(
        start(copy(wu, w_far.at[:, pl.ds(width, width)], x_send.at[3], x_recv.at[3], x_peer))
    )
    down_copy = start(copy(wd, wd_far, x_send.at[4], x_recv.at[4], x_peer))

    tile = 4 * half
    blocks = 4

    def rows_of(i):
        return pl.ds(pl.multiple_of(i * tile, tile), tile)

    def scale_rows(h, i):
        rows, group = rows_of(i), pl.ds(i * 4, 4)
        lanes = lax.broadcasted_iota(jnp.int32, (tile, table.shape[-1]), 1)
        column = jnp.sum(
            jnp.where(lanes == e, table[group].reshape(tile, -1), 0.0), axis=1, keepdims=True
        )
        value = acts[h, group, 1].reshape(tile, feats).astype(jnp.float32)
        scaled[h, rows, :] = (value * column).astype(jnp.bfloat16)

    def near_rows(first, count):
        @pl.loop(first, first + count)
        def _(i):
            left = acts[0, pl.ds(i * 4, 4), 0].reshape(tile, feats)
            pre[rows_of(i), :] = jnp.dot(left, w_own[...], preferred_element_type=jnp.float32)
            scale_rows(0, i)
            back_near[rows_of(i), :] = contract_cols(scaled[0, rows_of(i), :], wd_own[...])

    for j in (1, 3, 2):
        for p in (2, 0):
            line_step(p, 0, j)
            start(y_copy(p, j))
            start(c_copy(p, j))
        if j == 3:
            y_copy(3, 0).wait_recv()
            line_start(3, 4)
            start(c_copy(3, 4))
    for j in (1, 3, 2):
        line_step(1, 0, j)
        start(y_copy(1, j))
        start(c_copy(1, j))
    for j in (0, 1, 3, 2):
        for p in (2, 0):
            y_copy(p, j).wait_recv()
            start(c_copy(p, 4 + j))
    for item in own_copies[2:]:
        item.wait()
    near_rows(0, 2)
    for p in (2, 0):
        for j in range(8):
            c_copy(p, j).wait_recv()
    near_rows(2, 2)
    for j in (1, 3, 2):
        for base in (0, 4):
            line_step(3, base, j)
            start(c_copy(3, base + j))
    for j in (0, 1, 3, 2):
        y_copy(1, j).wait_recv()
        start(c_copy(1, 4 + j))
    for j in range(8):
        c_copy(1, j).wait_recv()
    for item in w_copies:
        item.wait_recv()

    @pl.loop(0, blocks)
    def _(i):
        rows = rows_of(i)
        left = acts[1, pl.ds(i * 4, 4), 0].reshape(tile, feats)
        total = pre[rows, :] + jnp.dot(left, w_far[...], preferred_element_type=jnp.float32)
        gate, up = total[:, :width], total[:, width:]
        sig = jax.nn.sigmoid(gate)
        hidden[rows, :] = (gate * sig * up).astype(jnp.bfloat16)
        pre[rows, :width] = up * sig * (1.0 + gate * (1.0 - sig))
        pre[rows, width:] = gate * sig

    for j in range(8):
        c_copy(3, j).wait_recv()

    @pl.loop(0, blocks)
    def _(i):
        scale_rows(1, i)

    strip = feats // 4

    def cols_of(i):
        return pl.ds(pl.multiple_of(i * strip, strip), strip)

    @pl.loop(0, 4)
    def _(i):
        down_send[:, cols_of(i)] = contract_first(hidden[...], scaled[1, :, cols_of(i)]).astype(jnp.bfloat16)

    grad_copies = [start(copy(down_send, down_far, x_send.at[5], x_recv.at[5], x_peer))]
    down_copy.wait_recv()

    @pl.loop(0, blocks)
    def _(i):
        rows = rows_of(i)
        back = back_near[rows, :] + contract_cols(scaled[1, rows, :], wd_far[...])
        d_both[rows, :width] = (back * pre[rows, :width]).astype(jnp.bfloat16)
        d_both[rows, width:] = (back * pre[rows, width:]).astype(jnp.bfloat16)

    chunk = feats // 2

    def rc_copy(h):
        return copy(row_grad.at[h, pl.ds(8, 8)], from_core.at[h], rc_send.at[h], rc_recv.at[h], core_peer)

    def ry_copy(h):
        return copy(row_grad.at[h, pl.ds(4, 4)], from_y.at[h], ry_send.at[h], ry_recv.at[h], y_peer)

    def rz_copy(h, k):
        return copy(row_grad.at[h, k], from_z.at[h, 3 - k], rz_send.at[h, k - 1], rz_recv.at[h, 3 - k], z_peers[k - 1])

    def rows_back(q, first):
        weights = w_own if q < 2 else w_far
        part = pl.ds(q % 2 * chunk, chunk)

        @pl.loop(first, first + 2)
        def _(i):
            value = contract_cols(d_both[rows_of(i), :], weights[part, :])
            row_grad[q, pl.ds(i * 4, 4)] = value.astype(jnp.bfloat16).reshape(4, half, chunk)

    def to_y(q):
        rows_back(q, 0)
        rc_copy(q).wait_recv()

        @pl.loop(4, 8)
        def _(j):
            near = row_grad[q, j].astype(jnp.float32)
            row_grad[q, j] = (near + from_core[q, j].astype(jnp.float32)).astype(jnp.bfloat16)

        start(ry_copy(q))

    def to_z(q):
        ry_copy(q).wait_recv()

        @pl.loop(0, 4)
        def _(j):
            near = row_grad[q, j].astype(jnp.float32) + from_core[q, j].astype(jnp.float32)
            row_grad[q, j] = (near + from_y[q, j].astype(jnp.float32)).astype(jnp.bfloat16)

        for k in (2, 1, 3):
            start(rz_copy(q, k))

    def finish(q):
        total = row_grad[q, 0].astype(jnp.float32)
        for k in range(3):
            rz_copy(q, 3 - k).wait_recv()
        for k in range(3):
            total = total + from_z[q, k].astype(jnp.float32)
        return total.astype(jnp.bfloat16)

    def far_grads(part):
        @pl.loop(2 * part, 2 * part + 2)
        def _(i):
            left = acts[1, :, 0, :, cols_of(i)].reshape(16 * half, strip)
            both_send[cols_of(i), :] = contract_first(left, d_both[...]).astype(jnp.bfloat16)

        rows = pl.ds(part * chunk, chunk)
        grad_copies.append(
            start(copy(both_send.at[rows], both_far.at[rows], x_send.at[6 + part], x_recv.at[6 + part], x_peer))
        )

    for q in (2, 3):
        rows_back(q, 2)
        start(rc_copy(q))
    to_y(2)
    far_grads(0)
    for q in (0, 1):
        rows_back(q, 2)
        start(rc_copy(q))
    to_y(3)
    far_grads(1)
    to_y(0)
    to_z(2)
    to_y(1)
    to_z(3)

    @pl.loop(0, 4)
    def _(i):
        left = acts[0, :, 0, :, cols_of(i)].reshape(16 * half, strip)
        both_own[cols_of(i), :] = contract_first(left, d_both[...])
        down_own[:, cols_of(i)] = contract_first(hidden[...], scaled[0, :, cols_of(i)])

    to_z(0)
    tok_send[:, :chunk] = finish(2)
    to_z(1)
    tok_send[:, chunk:] = finish(3)
    tok_copy = start(copy(tok_send, tok_far, x_send.at[8], x_recv.at[8], x_peer))
    grad_copies[0].wait_recv()
    out_down[...] = (down_own[...] + down_far[...].astype(jnp.float32)).astype(jnp.bfloat16)
    out_tok[mine, :chunk] = finish(0)
    out_tok[mine, chunk:] = finish(1)
    for part in range(2):
        rows = pl.ds(part * chunk, chunk)
        grad_copies[1 + part].wait_recv()
        total = (both_own[rows, :] + both_far[rows, :].astype(jnp.float32)).astype(jnp.bfloat16)
        out_gate[rows, :] = total[:, :width]
        out_up[rows, :] = total[:, width:]
    tok_copy.wait_recv()
    out_tok[theirs, :] = tok_far[...]
    for item in sends:
        item.wait_send()
    for condition, item in guarded:
        pl.when(condition)(item.wait_send)


def copy_kernel(*refs):
    ins, outs, held = refs[0:4], refs[4:8], refs[8:12]
    arrive, leave = refs[12:]
    reads = [pltpu.make_async_copy(ins[i], held[i], arrive.at[i]) for i in range(4)]
    writes = [pltpu.make_async_copy(held[i], outs[i], leave.at[i]) for i in range(4)]
    for item in reads:
        item.start()
    for i in range(4):
        reads[i].wait()
        writes[i].start()
    for item in writes:
        item.wait()


def dense_shards(tokens, grad_out, routes, gates, w_gate, w_up, w_down):
    experts = lax.axis_size("expert")
    tok_count, feats = tokens.shape
    width = w_gate.shape[2]
    half = tok_count // 2
    bf, f32 = jnp.bfloat16, jnp.float32
    rows = experts * half
    vmem = pl.BlockSpec(memory_space=pltpu.VMEM)
    anywhere = pl.BlockSpec(memory_space=pl.ANY)
    dma = pltpu.SemaphoreType.DMA
    results = pl.pallas_call(
        fused_kernel,
        out_shape=(
            jax.ShapeDtypeStruct((tok_count, feats), bf),
            jax.ShapeDtypeStruct((feats, width), bf),
            jax.ShapeDtypeStruct((feats, width), bf),
            jax.ShapeDtypeStruct((width, feats), bf),
        ),
        in_specs=[anywhere] * 2 + [vmem] * 2 + [anywhere] * 3,
        out_specs=(vmem,) * 4,
        scratch_shapes=[
            pltpu.VMEM((2, experts, 2, half, feats), bf),
            pltpu.VMEM((experts, half, 128), f32),
            pltpu.VMEM((feats, 2 * width), bf),
            pltpu.VMEM((feats, 2 * width), bf),
            pltpu.VMEM((width, feats), bf),
            pltpu.VMEM((2, rows, feats), bf),
            pltpu.VMEM((rows, 2 * width), f32),
            pltpu.VMEM((rows, width), bf),
            pltpu.VMEM((rows, 2 * width), bf),
            pltpu.VMEM((4, experts, half, feats // 2), bf),
            pltpu.VMEM((4, 8, half, feats // 2), bf),
            pltpu.VMEM((4, 4, half, feats // 2), bf),
            pltpu.VMEM((4, 3, half, feats // 2), bf),
            pltpu.VMEM((half, feats), bf),
            pltpu.VMEM((half, feats), bf),
            pltpu.VMEM((feats, 2 * width), f32),
            pltpu.VMEM((width, feats), f32),
            pltpu.VMEM((feats, 2 * width), bf),
            pltpu.VMEM((width, feats), bf),
            pltpu.VMEM((feats, 2 * width), bf),
            pltpu.VMEM((width, feats), bf),
            pltpu.VMEM(routes.shape, jnp.int32),
            pltpu.VMEM(gates.shape, f32),
            pltpu.VMEM((rows, width), f32),
            pltpu.VMEM((width, feats), bf),
            dma((5,)),
            dma((9,)), dma((9,)),
            dma((4, 2, 5)), dma((4, 2, 3)),
            dma((4, 4)), dma((4, 4)),
            dma((4, 8)), dma((4, 8)),
            dma((4,)), dma((4,)),
            dma((4,)), dma((4,)),
            dma((4, 3)), dma((4, 3)),
        ],
        compiler_params=pltpu.CompilerParams(
            collective_id=0, has_side_effects=True, vmem_limit_bytes=60 * 1024 * 1024
        ),
        cost_estimate=pl.CostEstimate(
            flops=16 * rows * 2 * feats * width, bytes_accessed=8 * 1024 * 1024, transcendentals=rows * width
        ),
    )(tokens, grad_out, routes.T, gates.T, w_gate[0], w_up[0], w_down[0])
    d_tokens, grad_gate, grad_up, grad_down = pl.pallas_call(
        copy_kernel,
        out_shape=tuple(jax.ShapeDtypeStruct(r.shape, r.dtype) for r in results),
        in_specs=[anywhere] * 4,
        out_specs=(anywhere,) * 4,
        scratch_shapes=[pltpu.VMEM(r.shape, r.dtype) for r in results] + [dma((4,)), dma((4,))],
        compiler_params=pltpu.CompilerParams(vmem_limit_bytes=60 * 1024 * 1024),
    )(*results)
    return (d_tokens, grad_gate[None], grad_up[None], grad_down[None])


def solution(mesh):
    small = mesh.shape["expert"] == 16 and mesh.shape["dp"] == 2
    return jax.shard_map(
        dense_shards if small else shards,
        mesh=mesh,
        in_specs=(
            P("expert", "dp"),
            P("expert", "dp"),
            P("expert", None),
            P("expert", None),
            P("expert", "dp", None),
            P("expert", "dp", None),
            P("expert", None, "dp"),
        ),
        out_specs=(
            P("expert", "dp"),
            P("expert", "dp", None),
            P("expert", "dp", None),
            P("expert", None, "dp"),
        ),
        check_vma=False,
    )
```

```python
import jax
import jax.numpy as jnp
from jax import lax
from jax.experimental import pallas as pl
from jax.experimental.pallas import tpu as pltpu
from jax.sharding import PartitionSpec as P


def contract_rows(left_rows, right_rows):
    return lax.dot_general(
        left_rows, right_rows, (((0,), (0,)), ((), ())), preferred_element_type=jnp.float32
    )


def contract_cols(left_rows, right_rows):
    return lax.dot_general(
        left_rows, right_rows, (((1,), (1,)), ((), ())), preferred_element_type=jnp.float32
    )


def per_source(left_rows, right_rows, dp_count):
    left_split = left_rows.reshape(dp_count, -1, left_rows.shape[1])
    right_split = right_rows.reshape(dp_count, -1, right_rows.shape[1])
    partial_value = jnp.einsum(
        "jra,jrb->jab", left_split, right_split, preferred_element_type=jnp.float32
    )
    rounded = lax.optimization_barrier(partial_value.astype(jnp.bfloat16))
    return jnp.sum(rounded.astype(jnp.float32), axis=0).astype(jnp.bfloat16)


def shards(tokens, grad_out, routes, gates, w_gate, w_up, w_down):
    experts = lax.axis_size("expert")
    dp_count = lax.axis_size("dp")
    tok_count = tokens.shape[0]
    top_count = routes.shape[1]
    slot_cap = min(tok_count, max(2, 3 * tok_count * top_count // (2 * experts)))
    row_total = tok_count * top_count
    flat_routes = routes.reshape(-1)
    flat_gates = gates.reshape(-1)
    onehot = (flat_routes[:, None] == jnp.arange(experts, dtype=jnp.int32)[None, :]).astype(
        jnp.int32
    )
    slot_rank = jnp.sum((jnp.cumsum(onehot, axis=0) - onehot) * onehot, axis=1)
    slot_index = flat_routes * slot_cap + slot_rank
    slot_source = (
        jnp.full((experts * slot_cap,), row_total, jnp.int32)
        .at[slot_index]
        .set(jnp.arange(row_total, dtype=jnp.int32))
    )
    valid = slot_source < row_total
    safe_rows = jnp.where(valid, slot_source, 0)
    token_ids = safe_rows // top_count
    token_slots = jnp.where(valid[:, None], tokens[token_ids], jnp.zeros((), tokens.dtype))
    scaled_slots = jnp.where(
        valid[:, None],
        grad_out[token_ids].astype(jnp.float32) * flat_gates[safe_rows][:, None],
        0.0,
    ).astype(jnp.bfloat16)
    input_cols, scaled_cols = (
        lax.all_to_all(token_slots, "expert", split_axis=0, concat_axis=0, tiled=True),
        lax.all_to_all(scaled_slots, "expert", split_axis=0, concat_axis=0, tiled=True),
    )
    inputs, scaled = (
        lax.all_to_all(input_cols, "dp", split_axis=0, concat_axis=1, tiled=True),
        lax.all_to_all(scaled_cols, "dp", split_axis=0, concat_axis=1, tiled=True),
    )
    full_gate, full_up, full_down = (
        lax.all_gather(w_gate, "dp", axis=1, tiled=True),
        lax.all_gather(w_up, "dp", axis=1, tiled=True),
        lax.all_gather(w_down, "dp", axis=2, tiled=True),
    )
    full_gate = full_gate[0]
    full_up = full_up[0]
    full_down = full_down[0]
    pre_gate = jnp.dot(inputs, full_gate, preferred_element_type=jnp.float32)
    pre_up = jnp.dot(inputs, full_up, preferred_element_type=jnp.float32)
    sigmoid_gate = jax.nn.sigmoid(pre_gate)
    activated = pre_gate * sigmoid_gate
    hidden = (activated * pre_up).astype(jnp.bfloat16)
    back_hidden = contract_cols(scaled, full_down)
    d_up = (back_hidden * activated).astype(jnp.bfloat16)
    d_gate = (back_hidden * pre_up * sigmoid_gate * (1.0 + pre_gate * (1.0 - sigmoid_gate))).astype(
        jnp.bfloat16
    )
    row_grad = (contract_cols(d_gate, full_gate) + contract_cols(d_up, full_up)).astype(
        jnp.bfloat16
    )
    came_back = lax.all_to_all(
        lax.all_to_all(row_grad, "dp", split_axis=1, concat_axis=0, tiled=True),
        "expert",
        split_axis=0,
        concat_axis=0,
        tiled=True,
    )
    picked = came_back[slot_index].astype(jnp.float32)
    d_tokens = jnp.sum(picked.reshape(tok_count, top_count, -1), axis=1).astype(jnp.bfloat16)
    hidden_all = lax.all_gather(hidden, "dp", axis=0, tiled=True)
    grad_down = per_source(hidden_all, scaled_cols, dp_count)
    gate_part = contract_rows(inputs, d_gate).astype(jnp.bfloat16).astype(jnp.float32)
    up_part = contract_rows(inputs, d_up).astype(jnp.bfloat16).astype(jnp.float32)
    gate_sum, up_sum = (
        lax.psum_scatter(
            gate_part.astype(jnp.bfloat16), "dp", scatter_dimension=0, tiled=True
        ).astype(jnp.float32),
        lax.psum_scatter(
            up_part.astype(jnp.bfloat16), "dp", scatter_dimension=0, tiled=True
        ).astype(jnp.float32),
    )
    grad_gate = gate_sum.astype(jnp.bfloat16)
    grad_up = up_sum.astype(jnp.bfloat16)
    return (d_tokens, grad_gate[None], grad_up[None], grad_down[None])


MESH_ID = pl.DeviceIdType.MESH


def contract_first(left, right):
    return lax.dot_general(left, right, (((0,), (0,)), ((), ())), preferred_element_type=jnp.float32)


def fused_kernel(
    tok, cot, routes, gates, wg, wu, wd,
    out_tok, out_gate, out_up, out_down,
    acts, table, w_own, w_far, wd_far, scaled, pre, hidden, d_both,
    row_grad, from_core, from_y, from_z, tok_send, tok_far,
    both_own, down_own, both_send, down_send, both_far, down_far, named_rows, gate_rows,
    back_near, wd_own, local_sem,
    x_send, x_recv, z_send, z_recv, y_send, y_recv, c_send, c_recv,
    rc_send, rc_recv, ry_send, ry_recv, rz_send, rz_recv,
):
    e = lax.axis_index("expert")
    d = lax.axis_index("dp")
    core = e % 2
    y_pos = (e // 2) % 2
    z_pos = e // 4
    half = tok.shape[0] // 2
    feats = tok.shape[1]
    width = wg.shape[1]
    x_peer = (e, 1 - d)
    core_peer = (e + 1 - 2 * core, d)
    y_peer = (e + 2 - 4 * y_pos, d)
    z_peers = [((z_pos + k) % 4 * 4 + e % 4, d) for k in (1, 2, 3)]

    def copy(src, dst, send, recv, peer):
        return pltpu.make_async_remote_copy(
            src_ref=src, dst_ref=dst, send_sem=send, recv_sem=recv, device_id=peer, device_id_type=MESH_ID
        )

    barrier = pltpu.get_barrier_semaphore()
    for peer in [x_peer, core_peer, y_peer] + z_peers:
        pl.semaphore_signal(barrier, inc=1, device_id=peer, device_id_type=MESH_ID)

    mine = pl.ds(pl.multiple_of(d * half, half), half)
    theirs = pl.ds(pl.multiple_of((1 - d) * half, half), half)
    own_copies = [
        pltpu.make_async_copy(src, dst, local_sem.at[i])
        for i, (src, dst) in enumerate(
            [
                (tok.at[mine], acts.at[0, 0, 0]),
                (cot.at[mine], acts.at[0, 0, 1]),
                (wg, w_own.at[:, pl.ds(0, width)]),
                (wu, w_own.at[:, pl.ds(width, width)]),
                (wd, wd_own),
            ]
        )
    ]
    for item in own_copies:
        item.start()
    lanes = lax.broadcasted_iota(jnp.int32, (half, table.shape[-1]), 1)
    named_rows[...] = jnp.transpose(routes[...])
    gate_rows[...] = jnp.transpose(gates[...])
    chosen, weight = named_rows[mine, :], gate_rows[mine, :]
    own_table = jnp.zeros((half, table.shape[-1]), jnp.float32)
    for k in range(routes.shape[0]):
        own_table += jnp.where(lanes == chosen[:, k : k + 1], weight[:, k : k + 1], 0.0)
    table[0] = own_table
    pl.semaphore_wait(barrier, 6)

    sends = []

    def start(item):
        item.start()
        sends.append(item)
        return item

    swap_tok = start(copy(tok.at[theirs], acts.at[1, 0, 0], x_send.at[0], x_recv.at[0], x_peer))
    swap_cot = start(copy(cot.at[theirs], acts.at[1, 0, 1], x_send.at[1], x_recv.at[1], x_peer))

    def piece(p, j):
        if p == 2:
            return table.at[j]
        return acts.at[0, j] if p == 0 else acts.at[1, j, p // 3]

    up_peer = ((z_pos + 1) % 4 * 4 + e % 4, d)
    down_peer = ((z_pos + 3) % 4 * 4 + e % 4, d)
    guarded = []

    def line_copy(p, base, src, dst, send, peer):
        return copy(
            piece(p, base + src),
            piece(p, base + dst),
            z_send.at[p, base // 4, send],
            z_recv.at[p, base // 4, dst - 1],
            peer,
        )

    def start_when(condition, item):
        pl.when(condition)(item.start)
        guarded.append((condition, item))

    def line_start(p, base):
        start_when(z_pos < 3, line_copy(p, base, 0, 3, 0, up_peer))
        start_when(z_pos > 0, line_copy(p, base, 0, 1, 1, down_peer))

    def line_step(p, base, j):
        line_copy(p, base, 0, j, 0, up_peer).wait_recv()
        if j == 1:
            start_when((z_pos > 0) & (z_pos < 3), line_copy(p, base, 1, 2, 2, down_peer))
        elif j == 3:
            start_when((z_pos > 0) & (z_pos < 3), line_copy(p, base, 3, 2, 3, up_peer))
        else:
            start_when(z_pos == 1, line_copy(p, base, 2, 3, 4, down_peer))
            start_when(z_pos == 2, line_copy(p, base, 2, 1, 4, up_peer))

    def y_copy(p, j):
        return copy(piece(p, j), piece(p, 4 + j), y_send.at[p, j], y_recv.at[p, j], y_peer)

    def c_copy(p, j):
        return copy(piece(p, j), piece(p, 8 + j), c_send.at[p, j], c_recv.at[p, j], core_peer)

    own_copies[0].wait()
    own_copies[1].wait()
    for p in (2, 0):
        line_start(p, 0)
        start(y_copy(p, 0))
        start(c_copy(p, 0))
    w_copies = [start(copy(wg, w_far.at[:, pl.ds(0, width)], x_send.at[2], x_recv.at[2], x_peer))]
    swap_tok.wait_recv()
    line_start(1, 0)
    start(y_copy(1, 0))
    start(c_copy(1, 0))
    swap_cot.wait_recv()
    start(y_copy(3, 0))
    line_start(3, 0)
    start(c_copy(3, 0))
    w_copies.append(
        start(copy(wu, w_far.at[:, pl.ds(width, width)], x_send.at[3], x_recv.at[3], x_peer))
    )
    down_copy = start(copy(wd, wd_far, x_send.at[4], x_recv.at[4], x_peer))

    tile = 4 * half
    blocks = 4

    def rows_of(i):
        return pl.ds(pl.multiple_of(i * tile, tile), tile)

    def scale_rows(h, i):
        rows, group = rows_of(i), pl.ds(i * 4, 4)
        lanes = lax.broadcasted_iota(jnp.int32, (tile, table.shape[-1]), 1)
        column = jnp.sum(
            jnp.where(lanes == e, table[group].reshape(tile, -1), 0.0), axis=1, keepdims=True
        )
        value = acts[h, group, 1].reshape(tile, feats).astype(jnp.float32)
        scaled[h, rows, :] = (value * column).astype(jnp.bfloat16)

    def near_rows(first, count):
        @pl.loop(first, first + count)
        def _(i):
            left = acts[0, pl.ds(i * 4, 4), 0].reshape(tile, feats)
            pre[rows_of(i), :] = jnp.dot(left, w_own[...], preferred_element_type=jnp.float32)
            scale_rows(0, i)
            back_near[rows_of(i), :] = contract_cols(scaled[0, rows_of(i), :], wd_own[...])

    for j in (1, 3, 2):
        for p in (2, 0):
            line_step(p, 0, j)
            start(y_copy(p, j))
            start(c_copy(p, j))
        if j == 3:
            y_copy(3, 0).wait_recv()
            line_start(3, 4)
            start(c_copy(3, 4))
    for j in (1, 3, 2):
        line_step(1, 0, j)
        start(y_copy(1, j))
        start(c_copy(1, j))
    for j in (0, 1, 3, 2):
        for p in (2, 0):
            y_copy(p, j).wait_recv()
            start(c_copy(p, 4 + j))
    for item in own_copies[2:]:
        item.wait()
    near_rows(0, 2)
    for p in (2, 0):
        for j in range(8):
            c_copy(p, j).wait_recv()
    near_rows(2, 2)
    for j in (1, 3, 2):
        for base in (0, 4):
            line_step(3, base, j)
            start(c_copy(3, base + j))
    for j in (0, 1, 3, 2):
        y_copy(1, j).wait_recv()
        start(c_copy(1, 4 + j))
    for j in range(8):
        c_copy(1, j).wait_recv()
    for item in w_copies:
        item.wait_recv()

    @pl.loop(0, blocks)
    def _(i):
        rows = rows_of(i)
        left = acts[1, pl.ds(i * 4, 4), 0].reshape(tile, feats)
        total = pre[rows, :] + jnp.dot(left, w_far[...], preferred_element_type=jnp.float32)
        gate, up = total[:, :width], total[:, width:]
        sig = jax.nn.sigmoid(gate)
        hidden[rows, :] = (gate * sig * up).astype(jnp.bfloat16)
        pre[rows, :width] = up * sig * (1.0 + gate * (1.0 - sig))
        pre[rows, width:] = gate * sig

    for j in range(8):
        c_copy(3, j).wait_recv()

    @pl.loop(0, blocks)
    def _(i):
        scale_rows(1, i)

    strip = feats // 4

    def cols_of(i):
        return pl.ds(pl.multiple_of(i * strip, strip), strip)

    @pl.loop(0, 4)
    def _(i):
        down_send[:, cols_of(i)] = contract_first(hidden[...], scaled[1, :, cols_of(i)]).astype(jnp.bfloat16)

    grad_copies = [start(copy(down_send, down_far, x_send.at[5], x_recv.at[5], x_peer))]
    down_copy.wait_recv()

    @pl.loop(0, blocks)
    def _(i):
        rows = rows_of(i)
        back = back_near[rows, :] + contract_cols(scaled[1, rows, :], wd_far[...])
        d_both[rows, :width] = (back * pre[rows, :width]).astype(jnp.bfloat16)
        d_both[rows, width:] = (back * pre[rows, width:]).astype(jnp.bfloat16)

    chunk = feats // 2

    def rc_copy(h):
        return copy(row_grad.at[h, pl.ds(8, 8)], from_core.at[h], rc_send.at[h], rc_recv.at[h], core_peer)

    def ry_copy(h):
        return copy(row_grad.at[h, pl.ds(4, 4)], from_y.at[h], ry_send.at[h], ry_recv.at[h], y_peer)

    def rz_copy(h, k):
        return copy(row_grad.at[h, k], from_z.at[h, 3 - k], rz_send.at[h, k - 1], rz_recv.at[h, 3 - k], z_peers[k - 1])

    def rows_back(q, first):
        weights = w_own if q < 2 else w_far
        part = pl.ds(q % 2 * chunk, chunk)

        @pl.loop(first, first + 2)
        def _(i):
            value = contract_cols(d_both[rows_of(i), :], weights[part, :])
            row_grad[q, pl.ds(i * 4, 4)] = value.astype(jnp.bfloat16).reshape(4, half, chunk)

    def to_y(q):
        rows_back(q, 0)
        rc_copy(q).wait_recv()

        @pl.loop(4, 8)
        def _(j):
            near = row_grad[q, j].astype(jnp.float32)
            row_grad[q, j] = (near + from_core[q, j].astype(jnp.float32)).astype(jnp.bfloat16)

        start(ry_copy(q))

    def to_z(q):
        ry_copy(q).wait_recv()

        @pl.loop(0, 4)
        def _(j):
            near = row_grad[q, j].astype(jnp.float32) + from_core[q, j].astype(jnp.float32)
            row_grad[q, j] = (near + from_y[q, j].astype(jnp.float32)).astype(jnp.bfloat16)

        for k in (2, 1, 3):
            start(rz_copy(q, k))

    def finish(q):
        total = row_grad[q, 0].astype(jnp.float32)
        for k in range(3):
            rz_copy(q, 3 - k).wait_recv()
        for k in range(3):
            total = total + from_z[q, k].astype(jnp.float32)
        return total.astype(jnp.bfloat16)

    def far_grads(part):
        @pl.loop(2 * part, 2 * part + 2)
        def _(i):
            left = acts[1, :, 0, :, cols_of(i)].reshape(16 * half, strip)
            both_send[cols_of(i), :] = contract_first(left, d_both[...]).astype(jnp.bfloat16)

        rows = pl.ds(part * chunk, chunk)
        grad_copies.append(
            start(copy(both_send.at[rows], both_far.at[rows], x_send.at[6 + part], x_recv.at[6 + part], x_peer))
        )

    for q in (2, 3):
        rows_back(q, 2)
        start(rc_copy(q))
    to_y(2)
    far_grads(0)
    for q in (0, 1):
        rows_back(q, 2)
        start(rc_copy(q))
    to_y(3)
    far_grads(1)
    to_y(0)
    to_z(2)
    to_y(1)
    to_z(3)

    @pl.loop(0, 4)
    def _(i):
        left = acts[0, :, 0, :, cols_of(i)].reshape(16 * half, strip)
        both_own[cols_of(i), :] = contract_first(left, d_both[...])
        down_own[:, cols_of(i)] = contract_first(hidden[...], scaled[0, :, cols_of(i)])

    to_z(0)
    tok_send[:, :chunk] = finish(2)
    to_z(1)
    tok_send[:, chunk:] = finish(3)
    tok_copy = start(copy(tok_send, tok_far, x_send.at[8], x_recv.at[8], x_peer))
    grad_copies[0].wait_recv()
    out_down[...] = (down_own[...] + down_far[...].astype(jnp.float32)).astype(jnp.bfloat16)
    out_tok[mine, :chunk] = finish(0)
    out_tok[mine, chunk:] = finish(1)
    for part in range(2):
        rows = pl.ds(part * chunk, chunk)
        grad_copies[1 + part].wait_recv()
        total = (both_own[rows, :] + both_far[rows, :].astype(jnp.float32)).astype(jnp.bfloat16)
        out_gate[rows, :] = total[:, :width]
        out_up[rows, :] = total[:, width:]
    tok_copy.wait_recv()
    out_tok[theirs, :] = tok_far[...]
    for item in sends:
        item.wait_send()
    for condition, item in guarded:
        pl.when(condition)(item.wait_send)


def copy_kernel(*refs):
    ins, outs, held = refs[0:4], refs[4:8], refs[8:12]
    arrive, leave = refs[12:]
    reads = [pltpu.make_async_copy(ins[i], held[i], arrive.at[i]) for i in range(4)]
    writes = [pltpu.make_async_copy(held[i], outs[i], leave.at[i]) for i in range(4)]
    for item in reads:
        item.start()
    for i in range(4):
        reads[i].wait()
        writes[i].start()
    for item in writes:
        item.wait()


def dense_shards(tokens, grad_out, routes, gates, w_gate, w_up, w_down):
    experts = lax.axis_size("expert")
    tok_count, feats = tokens.shape
    width = w_gate.shape[2]
    half = tok_count // 2
    bf, f32 = jnp.bfloat16, jnp.float32
    rows = experts * half
    vmem = pl.BlockSpec(memory_space=pltpu.VMEM)
    anywhere = pl.BlockSpec(memory_space=pl.ANY)
    dma = pltpu.SemaphoreType.DMA
    results = pl.pallas_call(
        fused_kernel,
        out_shape=(
            jax.ShapeDtypeStruct((tok_count, feats), bf),
            jax.ShapeDtypeStruct((feats, width), bf),
            jax.ShapeDtypeStruct((feats, width), bf),
            jax.ShapeDtypeStruct((width, feats), bf),
        ),
        in_specs=[anywhere] * 2 + [vmem] * 2 + [anywhere] * 3,
        out_specs=(vmem,) * 4,
        scratch_shapes=[
            pltpu.VMEM((2, experts, 2, half, feats), bf),
            pltpu.VMEM((experts, half, 128), f32),
            pltpu.VMEM((feats, 2 * width), bf),
            pltpu.VMEM((feats, 2 * width), bf),
            pltpu.VMEM((width, feats), bf),
            pltpu.VMEM((2, rows, feats), bf),
            pltpu.VMEM((rows, 2 * width), f32),
            pltpu.VMEM((rows, width), bf),
            pltpu.VMEM((rows, 2 * width), bf),
            pltpu.VMEM((4, experts, half, feats // 2), bf),
            pltpu.VMEM((4, 8, half, feats // 2), bf),
            pltpu.VMEM((4, 4, half, feats // 2), bf),
            pltpu.VMEM((4, 3, half, feats // 2), bf),
            pltpu.VMEM((half, feats), bf),
            pltpu.VMEM((half, feats), bf),
            pltpu.VMEM((feats, 2 * width), f32),
            pltpu.VMEM((width, feats), f32),
            pltpu.VMEM((feats, 2 * width), bf),
            pltpu.VMEM((width, feats), bf),
            pltpu.VMEM((feats, 2 * width), bf),
            pltpu.VMEM((width, feats), bf),
            pltpu.VMEM(routes.shape, jnp.int32),
            pltpu.VMEM(gates.shape, f32),
            pltpu.VMEM((rows, width), f32),
            pltpu.VMEM((width, feats), bf),
            dma((5,)),
            dma((9,)), dma((9,)),
            dma((4, 2, 5)), dma((4, 2, 3)),
            dma((4, 4)), dma((4, 4)),
            dma((4, 8)), dma((4, 8)),
            dma((4,)), dma((4,)),
            dma((4,)), dma((4,)),
            dma((4, 3)), dma((4, 3)),
        ],
        compiler_params=pltpu.CompilerParams(
            collective_id=0, has_side_effects=True, vmem_limit_bytes=48 * 1024 * 1024
        ),
        cost_estimate=pl.CostEstimate(
            flops=16 * rows * 2 * feats * width, bytes_accessed=8 * 1024 * 1024, transcendentals=rows * width
        ),
    )(tokens, grad_out, routes.T, gates.T, w_gate[0], w_up[0], w_down[0])
    d_tokens, grad_gate, grad_up, grad_down = pl.pallas_call(
        copy_kernel,
        out_shape=tuple(jax.ShapeDtypeStruct(r.shape, r.dtype) for r in results),
        in_specs=[anywhere] * 4,
        out_specs=(anywhere,) * 4,
        scratch_shapes=[pltpu.VMEM(r.shape, r.dtype) for r in results] + [dma((4,)), dma((4,))],
        compiler_params=pltpu.CompilerParams(vmem_limit_bytes=8 * 1024 * 1024),
    )(*results)
    return (d_tokens, grad_gate[None], grad_up[None], grad_down[None])


def solution(mesh):
    small = mesh.shape["expert"] == 16 and mesh.shape["dp"] == 2
    return jax.shard_map(
        dense_shards if small else shards,
        mesh=mesh,
        in_specs=(
            P("expert", "dp"),
            P("expert", "dp"),
            P("expert", None),
            P("expert", None),
            P("expert", "dp", None),
            P("expert", "dp", None),
            P("expert", None, "dp"),
        ),
        out_specs=(
            P("expert", "dp"),
            P("expert", "dp", None),
            P("expert", "dp", None),
            P("expert", None, "dp"),
        ),
        check_vma=False,
    )
```
